32 devices in a mesh: out: 4 (over z), in: 8 (over y, x, core).
Axes of the slice: x: 2, y: 2, z: 4, core: 2. Of those that a mesh axis runs over, the one named last changes fastest.
Arguments:
- markov: bfloat16 [63, 2048, 2048], P(None, 'out', 'in'), may hold values from -0.03125 to 0.03125
- probes: bfloat16 [128, 32, 2048], P('out', None, 'in'), may hold values from -6 to 6
- pattern: int32 [32, 16], P('out', 'in'), may hold values 0 or 1
Outputs:
- sketch: bfloat16 [32, 2048, 128], P(None, 'out')
- corange: float32 [128, 32, 2048], P('out', None, 'in')
- gram_matrix: float32 [128, 128], replicated
The draws below stay inside these ranges and needn't reach their ends.
All inputs are finite; a program needn't handle non-finite values. No bound on the sum of `pattern` on one device may be relied on, other than what follows from the above.
Results may differ from the reference program's by a relative error of at most 0.015.
Values may be sent and summed in bfloat16 or wider, within the bound.
No kernel may reach another device: no remote copies, remote signals or barrier semaphores. Data moves between devices by JAX's collectives and lax.ppermute only.
A program may use at most 128 MiB of HBM per device.

```python
import jax
import jax.numpy as jnp
from jax import lax

OUTPUT_CHANNELS = 2048
M = 2048
S = 128
BO = 64
BI = 128
R = 32
C = 32
LAGS = 63


def set_ends(array, own_key, least, high):
    spot = [jax.random.randint(jax.random.fold_in(own_key, axis), (), 0, length) for axis, length in enumerate(array.shape)]
    widest = array.shape.index(max(array.shape))
    next_to = spot[:widest] + [(spot[widest] + 1) % array.shape[widest]] + spot[widest + 1:]
    return array.at[tuple(spot)].set(least).at[tuple(next_to)].set(high)


def levels(rng, extent, cuts, low, largest):
    def one(axis_at, parts):
        draws = jax.random.uniform(jax.random.fold_in(jax.random.fold_in(rng, 6), axis_at), (parts,), jnp.float32, low / len(cuts), largest / len(cuts))
        return jnp.repeat(jnp.exp(draws), extent[axis_at] // parts).reshape((-1,) + (1,) * (len(extent) - axis_at - 1))

    factor_of = one(*cuts[0])
    for cut in cuts[1:]:
        factor_of = factor_of * one(*cut)
    return factor_of


def normal_values(key, dims, deviation, most, cuts=(), kind=jnp.bfloat16):
    gain = levels(key, dims, cuts, -0.22, 0.18) if cuts else 1.0
    array = jax.random.normal(key, dims, jnp.float32) * deviation * gain
    return jnp.minimum(jnp.maximum(array, -most), most).astype(kind)


def setup_inputs(seed: int = 0) -> dict:
    seeds = jax.random.split(jax.random.key(seed), 4)
    return {
        "markov": normal_values(seeds[0], (LAGS, OUTPUT_CHANNELS, M), (C * M // 2) ** -0.5, 0.03125, ((1, 4), (2, 8))),
        "probes": normal_values(seeds[1], (S, C, M), 1.0, 6.0, ((0, 4), (2, 8))),
        "pattern": set_ends((jax.random.randint(seeds[2], (OUTPUT_CHANNELS // BO, M // BI), 0, 2) < 1).astype(jnp.int32), jax.random.fold_in(seeds[2], 1), 0, 1),
    }


def reference(markov, probes, pattern):
    keeper = jnp.repeat(jnp.repeat(pattern, BO, axis=0), BI, axis=1).astype(jnp.bfloat16)
    masked = (markov * keeper[None]).astype(jnp.float32)
    panel_list = probes.astype(jnp.float32)

    def sketch_row(lag_row):
        window_span = lax.dynamic_slice_in_dim(masked, lag_row, C, 0)
        return jnp.einsum("wby,gwy->bg", window_span, panel_list, precision=lax.Precision.HIGHEST)

    raw = lax.map(sketch_row, jnp.arange(R, dtype=jnp.int32))
    sketch = raw.astype(jnp.bfloat16)
    sketch_wide = sketch.astype(jnp.float32)
    gram_matrix = jnp.einsum("ips,ipt->st", sketch_wide, sketch_wide, precision=lax.Precision.HIGHEST) / (R * OUTPUT_CHANNELS)

    def corange_col(lag_col):
        window_span = lax.dynamic_slice_in_dim(masked, lag_col, R, 0)
        return jnp.einsum("ipm,ips->sm", window_span, sketch_wide, precision=lax.Precision.HIGHEST)

    stacked_rows = lax.map(corange_col, jnp.arange(C, dtype=jnp.int32))
    corange = jnp.moveaxis(stacked_rows, 0, 1)
    return sketch, corange, gram_matrix
```

```python
import functools

import jax
import jax.numpy as jnp
import ml_dtypes
import numpy as np
from jax import lax
from jax.experimental import pallas as pl
from jax.experimental.pallas import tpu as pltpu
from jax.sharding import PartitionSpec as P

OUTPUT_CHANNELS = 2048
BO = 64
BI = 128
R = 32
C = 32
LAGS = 63
F = 32
PARTS = 2
VMEM = 60 << 20

bf16 = jnp.bfloat16
f32 = jnp.float32


def split(a):
    hi = a.astype(ml_dtypes.bfloat16)
    lo = (a - hi.astype(np.float64)).astype(ml_dtypes.bfloat16)
    return np.concatenate([hi, lo], axis=0)


def constants():
    theta = np.pi * (2 * np.arange(F)[:, None] + 1) / 64
    lag = np.arange(64)[None]
    cos, sin = np.cos(theta * lag), np.sin(theta * lag)
    eye = np.eye(8)
    fwd = np.stack([cos, sin])
    lag_mat = np.einsum("cfk,pq->cfpkq", fwd, eye).reshape(2 * F * 8, 64 * 8)
    half = fwd[:, :, :32]
    probe_mat = np.einsum("cfj,pq->cfpqj", half, eye).reshape(2 * F * 8, 32 * 8)
    sketch_mat = np.einsum("cfj,pq->cfpjq", half, eye).reshape(2 * F * 8, 32 * 8)
    back = half / F
    raw_mat = np.einsum("cfi,pq->ipcfq", back, eye).reshape(32 * 8, 2 * F * 8)
    cor_mat = np.einsum("cfj,pq->pjcfq", back, eye).reshape(32 * 8, 2 * F * 8)
    return [split(a) for a in (lag_mat, probe_mat, sketch_mat, raw_mat, cor_mat)]


def both(mat_ref, x):
    y = jnp.dot(mat_ref[...], x, preferred_element_type=f32)
    n = y.shape[0] // 2
    return y[:n] + y[n:]


def lag_kernel(keep_ref, mat_ref, x_ref, o_ref):
    rows, m = x_ref.shape[1], x_ref.shape[2]
    keep = keep_ref[0].astype(f32)

    def body(b, _):
        at = pl.ds(pl.multiple_of(b * 16, 16), 16)
        x = x_ref[:, at, :].astype(f32) * keep[None]
        res = []
        for h in range(2):
            part = x[:, 8 * h : 8 * h + 8, :].reshape(LAGS * 8, m)
            part = jnp.concatenate([part, jnp.zeros((8, m), f32)], axis=0)
            res.append(both(mat_ref, part.astype(bf16)).reshape(2, F, 8, m))
        y = jnp.concatenate(res, axis=2).astype(bf16)
        o_ref[:, at, 0:m] = y[0]
        o_ref[:, at, m : 2 * m] = y[1]
        return 0

    lax.fori_loop(0, rows // 16, body, 0)


def lag_transform(markov, pattern, mat):
    lags, p, m = markov.shape
    keep = jnp.repeat(pattern, BI, axis=1).astype(f32)[:, None, :]
    return pl.pallas_call(
        lag_kernel,
        grid=(p // BO,),
        in_specs=[
            pl.BlockSpec((1, 1, m), lambda i: (i, 0, 0)),
            pl.BlockSpec(mat.shape, lambda i: (0, 0)),
            pl.BlockSpec((lags, BO, m), lambda i: (0, i, 0)),
        ],
        out_specs=pl.BlockSpec((F, BO, 2 * m), lambda i: (0, i, 0)),
        out_shape=jax.ShapeDtypeStruct((F, p, 2 * m), bf16),
        compiler_params=pltpu.CompilerParams(vmem_limit_bytes=VMEM),
        cost_estimate=pl.CostEstimate(
            flops=2 * p * m * 1024 * 64, bytes_accessed=4 * 64 * p * m, transcendentals=0
        ),
        name="lag_transform",
    )(keep, mat, markov)


def rotate_into(hat_ref, y, at, at2, lo, hi):
    c, s = y[0].astype(bf16), y[1].astype(bf16)
    hat_ref[:, at, lo] = c
    hat_ref[:, at2, hi] = c
    hat_ref[:, at, hi] = s
    hat_ref[:, at2, lo] = -s


def sketch_kernel(fwd_ref, back_ref, u_ref, m_ref, o_ref, hat, freq):
    step = pl.program_id(0)
    s_count, m = u_ref.shape[0], u_ref.shape[2]
    p = m_ref.shape[1]

    @pl.when(step == 0)
    def _():
        def body(b, _):
            res = []
            for h in range(2):
                x = u_ref[pl.ds(b * 16 + 8 * h, 8)].reshape(8 * C, m)
                res.append(both(fwd_ref, x).reshape(2, F, 8, m))
            y = jnp.concatenate(res, axis=2)
            at = pl.ds(pl.multiple_of(b * 16, 16), 16)
            at2 = pl.ds(pl.multiple_of(s_count + b * 16, 16), 16)
            rotate_into(hat, y, at, at2, slice(0, m), slice(m, 2 * m))
            return 0

        lax.fori_loop(0, s_count // 16, body, 0)

    freq[step] = lax.dot_general(
        hat[step], m_ref[0], (((1,), (1,)), ((), ())), preferred_element_type=f32
    )

    @pl.when(step == F - 1)
    def _():
        width = min(p, 256)

        def body(b, _):
            at = pl.ds(pl.multiple_of(b * 16, 16), 16)
            for w in range(p // width):
                cols = slice(w * width, (w + 1) * width)
                res = []
                for h in range(2):
                    x = back_input(freq, b, h, s_count, cols)
                    res.append(both(back_ref, x).reshape(R, 8, width))
                o_ref[:, at, cols] = jnp.concatenate(res, axis=1).astype(bf16)
            return 0

        lax.fori_loop(0, s_count // 16, body, 0)


def back_input(freq, b, h, s_count, cols):
    re = freq[:, pl.ds(pl.multiple_of(b * 16 + 8 * h, 8), 8), cols]
    im = freq[:, pl.ds(pl.multiple_of(s_count + b * 16 + 8 * h, 8), 8), cols]
    x = jnp.concatenate([re, im], axis=0)
    return x.reshape(2 * F * 8, x.shape[-1]).astype(bf16)


def sketch_part(probes, hankel, fwd, back):
    s_count, _, m = probes.shape
    p = hankel.shape[1]
    return pl.pallas_call(
        sketch_kernel,
        grid=(F,),
        in_specs=[
            pl.BlockSpec(fwd.shape, lambda f: (0, 0)),
            pl.BlockSpec(back.shape, lambda f: (0, 0)),
            pl.BlockSpec(probes.shape, lambda f: (0, 0, 0)),
            pl.BlockSpec((1, p, 2 * m), lambda f: (f, 0, 0)),
        ],
        out_specs=pl.BlockSpec((R, s_count, p), lambda f: (0, 0, 0)),
        out_shape=jax.ShapeDtypeStruct((R, s_count, p), bf16),
        scratch_shapes=[
            pltpu.VMEM((F, 2 * s_count, 2 * m), bf16),
            pltpu.VMEM((F, 2 * s_count, p), f32),
        ],
        compiler_params=pltpu.CompilerParams(vmem_limit_bytes=VMEM),
        cost_estimate=pl.CostEstimate(
            flops=2 * F * 256 * 2 * m * p * 2, bytes_accessed=4 * F * p * m, transcendentals=0
        ),
        name="sketch_part",
    )(fwd, back, probes, hankel)


def corange_kernel(fwd_ref, back_ref, k_ref, m_ref, o_ref, hat, freq):
    step = pl.program_id(0)
    s_count, p = k_ref.shape[1], k_ref.shape[2]
    m = m_ref.shape[2] // 2

    @pl.when(step == 0)
    def _():
        width = min(p, 256)

        def body(b, _):
            at = pl.ds(pl.multiple_of(b * 16, 16), 16)
            at2 = pl.ds(pl.multiple_of(s_count + b * 16, 16), 16)
            for w in range(p // width):
                k = k_ref[:, at, w * width : (w + 1) * width].astype(f32)
                res = []
                for h in range(2):
                    x = k[:, 8 * h : 8 * h + 8, :].reshape(R * 8, width).astype(bf16)
                    res.append(both(fwd_ref, x).reshape(2, F, 8, width))
                y = jnp.concatenate(res, axis=2)
                lo = slice(w * width, (w + 1) * width)
                hi = slice(p + w * width, p + (w + 1) * width)
                rotate_into(hat, y, at, at2, lo, hi)
            return 0

        lax.fori_loop(0, s_count // 16, body, 0)

    left = hat[step]
    freq[step] = jnp.dot(left[:, :p], m_ref[0, :, :m], preferred_element_type=f32) + jnp.dot(
        left[:, p:], m_ref[0, :, m:], preferred_element_type=f32
    )

    @pl.when(step == F - 1)
    def _():
        def body(b, _):
            for h in range(2):
                x = back_input(freq, b, h, s_count, slice(0, m))
                y = both(back_ref, x).reshape(8, C, m)
                o_ref[pl.ds(b * 16 + 8 * h, 8)] = y.astype(bf16)
            return 0

        lax.fori_loop(0, s_count // 16, body, 0)


def corange_part(sketch, hankel, fwd, back):
    _, s_count, p = sketch.shape
    m = hankel.shape[2] // 2
    return pl.pallas_call(
        corange_kernel,
        grid=(F,),
        in_specs=[
            pl.BlockSpec(fwd.shape, lambda f: (0, 0)),
            pl.BlockSpec(back.shape, lambda f: (0, 0)),
            pl.BlockSpec(sketch.shape, lambda f: (0, 0, 0)),
            pl.BlockSpec((1, p, 2 * m), lambda f: (f, 0, 0)),
        ],
        out_specs=pl.BlockSpec((s_count, C, m), lambda f: (0, 0, 0)),
        out_shape=jax.ShapeDtypeStruct((s_count, C, m), bf16),
        scratch_shapes=[
            pltpu.VMEM((F, 2 * s_count, 2 * p), bf16),
            pltpu.VMEM((F, 2 * s_count, m), f32),
        ],
        compiler_params=pltpu.CompilerParams(vmem_limit_bytes=VMEM),
        cost_estimate=pl.CostEstimate(
            flops=2 * F * 256 * 2 * m * p * 2, bytes_accessed=4 * F * p * m, transcendentals=0
        ),
        name="corange_part",
    )(fwd, back, sketch, hankel)


def swap(x, bit, n):
    return lax.ppermute(x, "in", [(d, d ^ (1 << bit)) for d in range(n)])


def halve(x, bit, n):
    side = (lax.axis_index("in") >> bit) & 1
    h = x.shape[0] // 2
    away = swap(lax.dynamic_slice_in_dim(x, (1 - side) * h, h).astype(bf16), bit, n)
    kept = lax.dynamic_slice_in_dim(x, side * h, h).astype(f32)
    return kept + away.astype(f32)


def double(x, bit, n):
    side = (lax.axis_index("in") >> bit) & 1
    other = swap(x, bit, n)
    return jnp.concatenate([jnp.where(side, other, x), jnp.where(side, x, other)], axis=0)


def sum_over_in(raw, n):
    rest = list(range(1, n.bit_length() - 1))
    kept = halve(raw, 0, n)
    h = kept.shape[0] // 2
    own, halves = [], []
    for x, order in ((kept[:h], rest), (kept[h:], rest[::-1])):
        for bit in order:
            x = halve(x, bit, n)
        x = x.astype(bf16)
        own.append(x)
        for bit in order[::-1]:
            x = double(x, bit, n)
        halves.append(x)
    side = lax.axis_index("in") & 1
    other = [swap(x, 0, n) for x in halves]
    low = [jnp.where(side, b, a) for a, b in zip(halves, other)]
    high = [jnp.where(side, a, b) for a, b in zip(halves, other)]
    return jnp.concatenate(low + high, axis=0), jnp.concatenate(own, axis=0)


def shards(n_out, n_in, mats, markov, probes, pattern):
    lag_mat, probe_mat, sketch_mat, raw_mat, cor_mat = [jnp.asarray(a) for a in mats]
    rows = probes.shape[0] // PARTS
    gathered = [
        lax.all_gather(probes[q * rows : (q + 1) * rows], "out", axis=0, tiled=True)
        for q in range(PARTS)
    ]
    hankel = lag_transform(markov, pattern, lag_mat)
    raws = [sketch_part(g, hankel, probe_mat, raw_mat) for g in gathered]
    sums = [sum_over_in(raw, n_in) for raw in raws]
    cors = [corange_part(full, hankel, sketch_mat, cor_mat) for full, _ in sums]
    parts = [lax.psum_scatter(c, "out", scatter_dimension=0, tiled=True) for c in cors]
    corange = jnp.concatenate(parts, axis=0).astype(f32)

    def in_order(blocks, axis):
        cut = [
            b.reshape(b.shape[:axis] + (n_out, 1, rows) + b.shape[axis + 1 :]) for b in blocks
        ]
        x = jnp.concatenate(cut, axis=axis + 1)
        return x.reshape(x.shape[:axis] + (n_out * PARTS * rows,) + x.shape[axis + 3 :])

    own = in_order([o for _, o in sums], 1)
    own, _ = lax.optimization_barrier((own, cors[-1]))
    local_gram = jnp.einsum("isp,itp->st", own, own, preferred_element_type=f32)
    gram_matrix = lax.psum(local_gram, ("out", "in")) / (R * OUTPUT_CHANNELS)
    full = in_order([f for f, _ in sums], 1)
    full, _ = lax.optimization_barrier((full, cors[-1]))
    sketch = jnp.swapaxes(full, 1, 2)
    return (sketch, corange, gram_matrix)


def solution(mesh):
    body = functools.partial(shards, mesh.shape["out"], mesh.shape["in"], constants())
    return jax.shard_map(
        body,
        mesh=mesh,
        in_specs=(P(None, "out", "in"), P("out", None, "in"), P("out", "in")),
        out_specs=(P(None, "out", None), P("out", None, "in"), P()),
        check_vma=False,
    )
```

```python
import functools

import jax
import jax.numpy as jnp
import ml_dtypes
import numpy as np
from jax import lax
from jax.experimental import pallas as pl
from jax.experimental.pallas import tpu as pltpu
from jax.sharding import PartitionSpec as P

OUTPUT_CHANNELS = 2048
BO = 64
BI = 128
R = 32
C = 32
LAGS = 63
F = 32
PARTS = 2
MARKOV_PARTS = 1
CHUNK = 4
VMEM = 60 << 20

bf16 = jnp.bfloat16
f32 = jnp.float32


def split(a):
    hi = a.astype(ml_dtypes.bfloat16)
    lo = (a - hi.astype(np.float64)).astype(ml_dtypes.bfloat16)
    return np.concatenate([hi, lo], axis=0)


def constants():
    theta = np.pi * (2 * np.arange(F)[:, None] + 1) / 64
    lag = np.arange(64)[None]
    cos, sin = np.cos(theta * lag), np.sin(theta * lag)
    eye = np.eye(8)
    fwd = np.stack([cos, sin])
    lag_mat = np.einsum("cfk,pq->cfpkq", fwd, eye).reshape(2 * F * 8, 64 * 8)
    half = fwd[:, :, :32]
    probe_mat = np.einsum("cfj,pq->cfpqj", half, eye).reshape(2 * F * 8, 32 * 8)
    sketch_mat = np.einsum("cfj,pq->cfpjq", half, eye).reshape(2 * F * 8, 32 * 8)
    back = half / F
    raw_mat = np.einsum("cfi,pq->ipcfq", back, eye).reshape(32 * 8, 2 * F * 8)
    cor_mat = np.einsum("cfj,pq->pjcfq", back, eye).reshape(32 * 8, 2 * F * 8)
    return [split(a) for a in (lag_mat, probe_mat, sketch_mat, raw_mat, cor_mat)]


def both(mat_ref, x):
    y = jnp.dot(mat_ref[...], x, preferred_element_type=f32)
    n = y.shape[0] // 2
    return y[:n] + y[n:]


def lag_kernel(keep_ref, mat_ref, x_ref, o_ref):
    rows, m = x_ref.shape[1], x_ref.shape[2]
    keep = keep_ref[0].astype(f32)

    def body(b, _):
        at = pl.ds(pl.multiple_of(b * 16, 16), 16)
        x = x_ref[:, at, :].astype(f32) * keep[None]
        res = []
        for h in range(2):
            part = x[:, 8 * h : 8 * h + 8, :].reshape(LAGS * 8, m)
            part = jnp.concatenate([part, jnp.zeros((8, m), f32)], axis=0)
            res.append(both(mat_ref, part.astype(bf16)).reshape(2, F, 8, m))
        y = jnp.concatenate(res, axis=2).astype(bf16)
        o_ref[:, at, 0:m] = y[0]
        o_ref[:, at, m : 2 * m] = y[1]
        return 0

    lax.fori_loop(0, rows // 16, body, 0)


def lag_transform(markov, keep, mat, part):
    lags, p, m = markov.shape
    blocks = p // BO // MARKOV_PARTS
    return pl.pallas_call(
        lag_kernel,
        grid=(blocks,),
        in_specs=[
            pl.BlockSpec((1, 1, m), lambda i: (part * blocks + i, 0, 0)),
            pl.BlockSpec(mat.shape, lambda i: (0, 0)),
            pl.BlockSpec((lags, BO, m), lambda i: (0, part * blocks + i, 0)),
        ],
        out_specs=pl.BlockSpec((F, BO, 2 * m), lambda i: (0, i, 0)),
        out_shape=jax.ShapeDtypeStruct((F, p // MARKOV_PARTS, 2 * m), bf16),
        compiler_params=pltpu.CompilerParams(vmem_limit_bytes=VMEM),
        cost_estimate=pl.CostEstimate(
            flops=p * m * 1024 * 64, bytes_accessed=2 * 64 * p * m, transcendentals=0
        ),
        name="lag_transform",
    )(keep, mat, markov)


def rotate_into(hat_ref, y, at, at2, lo, hi):
    c, s = y[0].astype(bf16), y[1].astype(bf16)
    hat_ref[:, at, lo] = c
    hat_ref[:, at2, hi] = c
    hat_ref[:, at, hi] = s
    hat_ref[:, at2, lo] = -s


def fetch(m_hbms, m_ref, sems):
    rows = m_ref.shape[1] // MARKOV_PARTS

    def copies(c):
        at = pl.ds(c * CHUNK, CHUNK)
        return [
            pltpu.make_async_copy(
                m_hbm.at[at], m_ref.at[at, pl.ds(k * rows, rows)], sems.at[k, c]
            )
            for k, m_hbm in enumerate(m_hbms)
        ]

    for c in range(F // CHUNK):
        for copy in copies(c):
            copy.start()
    return copies


def over_frequencies(copies, one):
    def body(c, _):
        for copy in copies(c):
            copy.wait()
        for k in range(CHUNK):
            one(c * CHUNK + k)
        return 0

    lax.fori_loop(0, F // CHUNK, body, 0)


def back_input(freq, b, h, s_count, cols):
    re = freq[:, pl.ds(pl.multiple_of(b * 16 + 8 * h, 8), 8), cols]
    im = freq[:, pl.ds(pl.multiple_of(s_count + b * 16 + 8 * h, 8), 8), cols]
    x = jnp.concatenate([re, im], axis=0)
    return x.reshape(2 * F * 8, x.shape[-1]).astype(bf16)


def sketch_kernel(n, n_out, n_in, place_ref, fwd_ref, back_ref, *refs):
    u_refs, m_hbms, refs = refs[:n], refs[n : n + MARKOV_PARTS], refs[n + MARKOV_PARTS :]
    sums, (back, m_ref, hat, freq, sems) = refs[: 2 * PARTS], refs[2 * PARTS :]
    whole = u_refs[n_out:]
    u_refs = list(u_refs[:n_out])
    for ref in whole:
        u_refs += [ref.at[lax.rem(place_ref[0] + d, n_out)] for d in range(n_out)]
    rows, _, m = u_refs[0].shape
    s_count, p = n_out * PARTS * rows, m_ref.shape[1]
    copies = fetch(m_hbms, m_ref, sems)

    for b in range(s_count // 16):
        res = []
        for g in (2 * b, 2 * b + 1):
            first = (g * 8) % rows
            x = u_refs[g * 8 // rows][first : first + 8].reshape(8 * C, m)
            res.append(both(fwd_ref, x).reshape(2, F, 8, m))
        y = jnp.concatenate(res, axis=2)
        at, at2 = pl.ds(b * 16, 16), pl.ds(s_count + b * 16, 16)
        rotate_into(hat, y, at, at2, slice(0, m), slice(m, 2 * m))

    def one(f):
        freq[f] = lax.dot_general(
            hat[f], m_ref[f], (((1,), (1,)), ((), ())), preferred_element_type=f32
        )

    over_frequencies(copies, one)
    width = min(p, 256)
    g = R // n_in * 8
    for part in range(2):
        for k, slot in enumerate(slots(n_in)):
            at = pl.ds(pl.multiple_of(part * R * 8 + (place_ref[1] ^ slot) * g, 16), g)
            back[part * R * 8 + k * g : part * R * 8 + (k + 1) * g] = back_ref[at]

    for q in range(PARTS):
        keep_ref, send_ref = sums[2 * q : 2 * q + 2]
        part = s_count // PARTS // 16

        def body(b, _):
            at = pl.ds(pl.multiple_of(b * 16, 16), 16)
            for w in range(p // width):
                cols = slice(w * width, (w + 1) * width)
                res = []
                for h in range(2):
                    x = back_input(freq, q * part + b, h, s_count, cols)
                    res.append(both(back, x).reshape(R, 8, width))
                y = jnp.concatenate(res, axis=1)
                keep_ref[:, at, cols] = y[: R // 2]
                send_ref[:, at, cols] = y[R // 2 :].astype(bf16)
            return 0

        lax.fori_loop(0, part, body, 0)


def vmem_specs(arrays):
    return [pl.BlockSpec(memory_space=pltpu.VMEM) for _ in arrays]


def any_specs(arrays):
    return [pl.BlockSpec(memory_space=pl.ANY) for _ in arrays]


def product_cost(p, m, extra):
    return pl.CostEstimate(
        flops=2 * F * 256 * 2 * m * p * 2, bytes_accessed=4 * F * p * m + extra, transcendentals=0
    )


def sketch_part(probes, hankel, fwd, back, place, n_out, n_in):
    rows, _, m = probes[0].shape
    p = hankel[0].shape[1] * MARKOV_PARTS
    part, s_count = rows * n_out, rows * n_out * PARTS
    return pl.pallas_call(
        functools.partial(sketch_kernel, len(probes), n_out, n_in),
        in_specs=[pl.BlockSpec(memory_space=pltpu.SMEM)]
        + vmem_specs([fwd, back, *probes])
        + any_specs(hankel),
        out_specs=vmem_specs(range(2 * PARTS)),
        out_shape=[
            jax.ShapeDtypeStruct((R // 2, part, p), f32),
            jax.ShapeDtypeStruct((R // 2, part, p), bf16),
        ]
        * PARTS,
        scratch_shapes=[
            pltpu.VMEM(back.shape, bf16),
            pltpu.VMEM((F, p, 2 * m), bf16),
            pltpu.VMEM((F, 2 * s_count, 2 * m), bf16),
            pltpu.VMEM((F, 2 * s_count, p), f32),
            pltpu.SemaphoreType.DMA((MARKOV_PARTS, F // CHUNK)),
        ],
        compiler_params=pltpu.CompilerParams(vmem_limit_bytes=VMEM),
        cost_estimate=product_cost(p, m, 0),
        name="sketch_part",
    )(place, fwd, back, *probes, *hankel)


def corange_kernel(n_in, n_out, n_before, n_o, place_ref, fwd_ref, back_ref, *refs):
    k_refs, refs = refs[: n_in // 2 + 1], refs[n_in // 2 + 1 :]
    m_hbms, refs = refs[:MARKOV_PARTS], refs[MARKOV_PARTS + n_before :]
    o_refs, (fwd, m_ref, hat, freq, sems) = refs[:n_o], refs[n_o:]
    if n_o == 1:
        o_refs = [o_refs[0].at[lax.rem(place_ref[0] + d, n_out)] for d in range(n_out)]
    _, s_count, p = k_refs[0].shape
    m = m_ref.shape[2] // 2
    rows = s_count // n_out
    copies = fetch(m_hbms, m_ref, sems)
    width = min(p, 256)

    g = R // n_in * 8
    to = lax.broadcasted_iota(jnp.int32, (R * 8, R * 8), 1)
    come = lax.broadcasted_iota(jnp.int32, (R * 8, R * 8), 0)
    where = to // g
    slot = jnp.where(where < n_in // 2, 2 * where, 2 * where - (n_in - 1))
    moved = come == (place_ref[1] ^ slot) * g + to % g
    move = jnp.where(moved, 1.0, 0.0).astype(bf16)
    fwd[...] = jnp.dot(fwd_ref[...], move, preferred_element_type=f32).astype(bf16)

    def forward(b, _):
        at = pl.ds(pl.multiple_of(b * 16, 16), 16)
        at2 = pl.ds(pl.multiple_of(s_count + b * 16, 16), 16)
        for w in range(p // width):
            cols = slice(w * width, (w + 1) * width)
            k = jnp.concatenate([ref[:, at, cols] for ref in k_refs], axis=0).astype(f32)
            res = []
            for h in range(2):
                x = k[:, 8 * h : 8 * h + 8, :].reshape(R * 8, width).astype(bf16)
                res.append(both(fwd, x).reshape(2, F, 8, width))
            y = jnp.concatenate(res, axis=2)
            lo = slice(w * width, (w + 1) * width)
            hi = slice(p + w * width, p + (w + 1) * width)
            rotate_into(hat, y, at, at2, lo, hi)
        return 0

    lax.fori_loop(0, s_count // 16, forward, 0)

    def one(f):
        left = hat[f]
        freq[f] = jnp.dot(left[:, :p], m_ref[f, :, :m], preferred_element_type=f32) + jnp.dot(
            left[:, p:], m_ref[f, :, m:], preferred_element_type=f32
        )

    over_frequencies(copies, one)

    for g in range(s_count // 8):
        x = back_input(freq, g // 2, g % 2, s_count, slice(0, m))
        first = (g * 8) % rows
        o_ref = o_refs[g * 8 // rows]
        o_ref[first : first + 8] = both(back_ref, x).reshape(8, C, m).astype(o_ref.dtype)


def corange_part(pieces, hankel, fwd, back, place, n_out, n_in, before, whole):
    _, s_count, p = pieces[0].shape
    m = hankel[0].shape[2] // 2
    rows = s_count // n_out
    if whole:
        outs = [jax.ShapeDtypeStruct((n_out, rows, C, m), bf16)]
    else:
        outs = [jax.ShapeDtypeStruct((rows, C, m), bf16 if d else f32) for d in range(n_out)]
    return pl.pallas_call(
        functools.partial(corange_kernel, n_in, n_out, len(before), len(outs)),
        in_specs=[pl.BlockSpec(memory_space=pltpu.SMEM)]
        + vmem_specs([fwd, back, *pieces])
        + any_specs([*hankel, *before]),
        out_specs=vmem_specs(outs),
        out_shape=outs,
        scratch_shapes=[
            pltpu.VMEM(fwd.shape, bf16),
            pltpu.VMEM((F, p, 2 * m), bf16),
            pltpu.VMEM((F, 2 * s_count, 2 * p), bf16),
            pltpu.VMEM((F, 2 * s_count, m), f32),
            pltpu.SemaphoreType.DMA((MARKOV_PARTS, F // CHUNK)),
        ],
        compiler_params=pltpu.CompilerParams(vmem_limit_bytes=VMEM),
        cost_estimate=product_cost(p, m, 0),
        name="corange_part",
    )(place, fwd, back, *pieces, *hankel, *before)


def in_order(x, both_parts, q, z, n_out):
    rows = x.shape[0] // n_out
    x = x.astype(f32)
    for d in range(n_out):
        first = lax.rem(z + d, n_out) * (PARTS * rows) + q * rows
        both_parts[pl.ds(pl.multiple_of(first, 8), rows), :] = x[d * rows : (d + 1) * rows]


def gram_kernel(n_out, place_ref, *refs):
    k_refs, (gram_ref, both_parts) = refs[:PARTS], refs[PARTS:]
    total = jnp.zeros(gram_ref.shape, f32)
    for i in range(k_refs[0].shape[0]):
        for q, ref in enumerate(k_refs):
            in_order(ref[i], both_parts, q, place_ref[0], n_out)
        x = both_parts[...].astype(bf16)
        total += lax.dot_general(x, x, (((1,), (1,)), ((), ())), preferred_element_type=f32)
    gram_ref[...] = total


def gram_part(own, place, n_out):
    _, s_count, p = own[0].shape
    s_count *= PARTS
    return pl.pallas_call(
        functools.partial(gram_kernel, n_out),
        in_specs=[pl.BlockSpec(memory_space=pltpu.SMEM)] + vmem_specs(own),
        out_specs=pl.BlockSpec(memory_space=pltpu.VMEM),
        out_shape=jax.ShapeDtypeStruct((s_count, s_count), f32),
        scratch_shapes=[pltpu.VMEM((s_count, p), f32)],
        name="gram_part",
    )(place, *own)


def total_kernel(n, *refs):
    done, rest, o_ref = refs[:n], refs[n:-2], refs[-1]
    rows = rest[0].shape[0]
    for q, ref in enumerate(done):
        o_ref[q * rows : (q + 1) * rows] = ref[...].astype(f32)
    total = rest[0][...]
    for ref in rest[1:]:
        total += ref[...].astype(f32)
    o_ref[n * rows :] = total


def total_corange(done, own, arrived, before):
    rows, *rest = own.shape
    return pl.pallas_call(
        functools.partial(total_kernel, len(done)),
        in_specs=vmem_specs([*done, own, *arrived]) + any_specs([before]),
        out_specs=pl.BlockSpec(memory_space=pltpu.VMEM),
        out_shape=jax.ShapeDtypeStruct((rows * PARTS, *rest), f32),
        name="total_corange",
    )(*done, own, *arrived, before)


def finish_kernel(n_out, n_in, place_ref, *refs):
    o_ref, both_parts = refs[-2:]
    n = n_in // 2 + 1
    i_count = refs[0].shape[0]
    z, idx = place_ref[0], place_ref[1]
    for k, slot in enumerate(slots(n_in)):
        ref, base = min(k, n - 1), max(k - (n - 1), 0) * i_count

        def body(t, _):
            for q in range(PARTS):
                in_order(refs[q * n + ref][base + t], both_parts, q, z, n_out)
            o_ref[(idx ^ slot) * i_count + t] = both_parts[...].T.astype(bf16)
            return 0

        lax.fori_loop(0, i_count, body, 0)


def finish(pieces, place, after, n_out, n_in):
    i_count, s_count, p = pieces[0][0].shape
    flat = [x for part in pieces for x in part]
    return pl.pallas_call(
        functools.partial(finish_kernel, n_out, n_in),
        in_specs=[pl.BlockSpec(memory_space=pltpu.SMEM)] + vmem_specs(flat) + any_specs(after),
        out_specs=pl.BlockSpec(memory_space=pltpu.VMEM),
        out_shape=jax.ShapeDtypeStruct((R, p, PARTS * s_count), bf16),
        scratch_shapes=[pltpu.VMEM((PARTS * s_count, p), f32)],
        compiler_params=pltpu.CompilerParams(vmem_limit_bytes=VMEM),
        cost_estimate=pl.CostEstimate(
            flops=0, bytes_accessed=16 * R * p * s_count, transcendentals=0
        ),
        name="finish",
    )(place, *flat, *after)


def slots(n):
    return [*range(0, n, 2), *range(1, n, 2)]


def to_xor(x, axis, r, n):
    return lax.ppermute(x, axis, [(d, d ^ r) for d in range(n)])


def settle_kernel(n, keep_ref, away_ref, *refs):
    total = keep_ref[...] + away_ref[...].astype(f32)
    for ref in refs[:n]:
        total += ref[...].astype(f32)
    refs[-1][...] = total.astype(bf16)


def settle(keep, away, arrived, before):
    block = pl.BlockSpec((1, *keep.shape[1:]), lambda i: (i, 0, 0))
    return pl.pallas_call(
        functools.partial(settle_kernel, len(arrived)),
        grid=(arrived[0].shape[0],),
        in_specs=[block] * (2 + len(arrived)) + any_specs(before),
        out_specs=block,
        out_shape=jax.ShapeDtypeStruct(arrived[0].shape, bf16),
        cost_estimate=pl.CostEstimate(
            flops=0, bytes_accessed=8 * arrived[0].size, transcendentals=0
        ),
        name="settle",
    )(keep, away, *arrived, *before)


def meet(keep, send, n):
    away = to_xor(send, "in", 1, n)
    g = R // n
    arrived = []
    for k in range(1, n // 2):
        rows = slice(k * g, (k + 1) * g)
        arrived.append(to_xor((keep[rows] + away[rows].astype(f32)).astype(bf16), "in", 2 * k, n))
    return keep, away, arrived


def spread(own, n):
    return [own] + [to_xor(own, "in", 2 * k, n) for k in range(1, n // 2)]


def join_kernel(n, *refs):
    rows = refs[0].shape[0]
    for k in range(n):
        refs[-1][k * rows : (k + 1) * rows] = refs[k][...]


def join(mine, before):
    rows, *rest = mine[0].shape
    return pl.pallas_call(
        functools.partial(join_kernel, len(mine)),
        in_specs=vmem_specs(mine) + any_specs(before),
        out_specs=pl.BlockSpec(memory_space=pltpu.VMEM),
        out_shape=jax.ShapeDtypeStruct((len(mine) * rows, *rest), bf16),
        name="join",
    )(*mine, *before)


def shards(n_out, n_in, mats, markov, probes, pattern):
    lag_mat, probe_mat, sketch_mat, raw_mat, cor_mat = [jnp.asarray(a) for a in mats]
    rows = probes.shape[0] // PARTS
    z, idx = lax.axis_index("out"), lax.axis_index("in")

    place = jnp.stack([z, idx]).astype(jnp.int32)
    keep = jnp.repeat(pattern, BI, axis=1).astype(f32)[:, None, :]

    own = probes[:rows]
    gathered = [own]
    for d in range(1, n_out):
        gathered.append(lax.ppermute(own, "out", [((k + d) % n_out, k) for k in range(n_out)]))
    for q in range(1, PARTS):
        gathered.append(lax.all_gather(probes[q * rows : (q + 1) * rows], "out"))
    hankel = [lag_transform(markov, keep, lag_mat, q) for q in range(MARKOV_PARTS)]

    raws = sketch_part(gathered, hankel, probe_mat, raw_mat, place, n_out, n_in)
    met = [meet(raws[2 * q], raws[2 * q + 1], n_in) for q in range(PARTS)]
    owns, sums, summed, before = [], [], [], []
    for q, x in enumerate(met):
        owns.append(settle(*x, before))
        mine = spread(owns[q], n_in)
        last = q == PARTS - 1
        gram = [gram_part(owns, place, n_out)] if last else []
        if last:
            for bit in range(n_in.bit_length() - 1):
                gram = [gram[0] + to_xor(gram[0], "in", 1 << bit, n_in)]
        sums.append(mine + [to_xor(join(mine, gram), "in", 1, n_in)])
        cor = corange_part(
            sums[q], hankel, sketch_mat, cor_mat, place, n_out, n_in, before, not last
        )
        before = [cor[-1]]
        if not last:
            whole = cor[0].reshape((-1,) + cor[0].shape[2:])
            summed.append(lax.psum_scatter(whole, "out", scatter_dimension=0, tiled=True))

    (gram,) = gram
    for bit in range(n_out.bit_length() - 1):
        gram = gram + to_xor(gram, "out", 1 << bit, n_out)
    gram_matrix = gram / (R * OUTPUT_CHANNELS)

    arrived = [
        lax.ppermute(cor[d], "out", [(k, (k + d) % n_out) for k in range(n_out)])
        for d in range(1, n_out)
    ]
    sketch = finish(sums, place, [*summed, *before, gram_matrix], n_out, n_in)
    corange = total_corange(summed, cor[0], arrived, sketch)
    return (sketch, corange, gram_matrix)


def solution(mesh):
    body = functools.partial(shards, mesh.shape["out"], mesh.shape["in"], constants())
    return jax.shard_map(
        body,
        mesh=mesh,
        in_specs=(P(None, "out", "in"), P("out", None, "in"), P("out", "in")),
        out_specs=(P(None, "out", None), P("out", None, "in"), P()),
        check_vma=False,
    )
```

```python
import functools

import jax
import jax.numpy as jnp
from jax import lax
from jax.experimental import pallas as pl
from jax.experimental.pallas import tpu as pltpu
from jax.sharding import PartitionSpec as P

OUTPUT_CHANNELS = 2048
BO = 64
BI = 128
R = 32
C = 32
LAGS = 63
PARTS = 2
VMEM = 60 << 20

bf16 = jnp.bfloat16
f32 = jnp.float32


def vmem_specs(arrays):
    return [pl.BlockSpec(memory_space=pltpu.VMEM) for _ in arrays]


def any_specs(arrays):
    return [pl.BlockSpec(memory_space=pl.ANY) for _ in arrays]


def steps_of(lags):
    return max(d for d in range(1, 8) if lags % d == 0)


def fetch(m_hbm, m_ref, sems):
    count = LAGS // sems.shape[0]
    copies = []
    for c in range(sems.shape[0]):
        at = pl.ds(c * count, count)
        copies.append(pltpu.make_async_copy(m_hbm.at[at], m_ref.at[at], sems.at[c]))
    for copy in copies:
        copy.start()

    def wait():
        for copy in copies:
            copy.wait()

    return wait


def product_cost(p, m, n):
    return pl.CostEstimate(
        flops=2 * R * C * p * m * n, bytes_accessed=2 * LAGS * p * m, transcendentals=0
    )


def sketch_kernel(n_out, n_in, place_ref, *refs):
    u_refs, (m_hbm, keep_ref, send_ref, m_ref, rows_ref, w_ref, acc, sems) = refs[:-8], refs[-8:]
    if len(u_refs) == 1:
        u_refs = [u_refs[0].at[lax.rem(place_ref[0] + d, n_out)] for d in range(n_out)]
    _, rows, m = u_refs[0].shape
    g = R // n_in
    s_count = rows * n_out
    width = g * s_count
    lags = C + g - 1
    wait = fetch(m_hbm, m_ref, sems)

    edge = (g - 1) * s_count
    rows_ref[:edge] = jnp.zeros((edge, m), bf16)
    rows_ref[edge + C * s_count :] = jnp.zeros((edge, m), bf16)
    for j in range(C):
        x = jnp.concatenate([ref[j] for ref in u_refs], axis=0)
        rows_ref[edge + j * s_count : edge + (j + 1) * s_count] = x

    def turn(t, _):
        x = rows_ref[pl.ds(pl.multiple_of(t * s_count, s_count), width), :]
        w_ref[t] = x.T
        return 0

    lax.fori_loop(0, lags, turn, 0)
    wait()
    count = steps_of(lags)

    def slot(k, _):
        for side, o_ref in enumerate((keep_ref, send_ref)):
            first = (place_ref[1] ^ (2 * k + side)) * g

            def some(t, _):
                total = jnp.zeros(acc.shape, f32)
                for q in range(count):
                    lag = t * count + q
                    total += jnp.dot(m_ref[first + lag], w_ref[lag], preferred_element_type=f32)

                @pl.when(t == 0)
                def _():
                    acc[...] = total

                @pl.when(t > 0)
                def _():
                    acc[...] += total

                return 0

            lax.fori_loop(0, lags // count, some, 0)
            o_ref[k] = acc[...].astype(o_ref.dtype)
        return 0

    lax.fori_loop(0, n_in // 2, slot, 0)


def sketch_part(probes, masked, place, n_out, n_in):
    _, rows, m = probes[0].shape[-3:]
    p = masked.shape[1]
    g, s_count = R // n_in, rows * n_out
    width, lags = g * s_count, C + g - 1
    return pl.pallas_call(
        functools.partial(sketch_kernel, n_out, n_in),
        in_specs=[pl.BlockSpec(memory_space=pltpu.SMEM)]
        + vmem_specs(probes)
        + any_specs([masked]),
        out_specs=vmem_specs(range(2)),
        out_shape=[
            jax.ShapeDtypeStruct((n_in // 2, p, width), f32),
            jax.ShapeDtypeStruct((n_in // 2, p, width), bf16),
        ],
        scratch_shapes=[
            pltpu.VMEM((LAGS, p, m), bf16),
            pltpu.VMEM(((C + 2 * (g - 1)) * s_count, m), bf16),
            pltpu.VMEM((lags, m, width), bf16),
            pltpu.VMEM((p, width), f32),
            pltpu.SemaphoreType.DMA((9,)),
        ],
        compiler_params=pltpu.CompilerParams(vmem_limit_bytes=VMEM),
        cost_estimate=pl.CostEstimate(flops=0, bytes_accessed=1, transcendentals=0),
        name="sketch_part",
    )(place, *probes, masked)


def corange_kernel(n_in, n_out, n_before, place_ref, *refs):
    n = n_in // 2 + 1
    k_refs, m_hbm, refs = refs[:n], refs[n], refs[n + 1 + n_before :]
    o_refs, (m_ref, rows_ref, acc, sems) = refs[:-4], refs[-4:]
    if len(o_refs) == 1:
        o_refs = [o_refs[0].at[lax.rem(place_ref[0] + d, n_out)] for d in range(n_out)]
    _, p, width = k_refs[0].shape
    g = R // n_in
    s_count = width // g
    rows = s_count // n_out
    lags = R + g - 1
    wait = fetch(m_hbm, m_ref, sems)

    edge = (g - 1) * s_count
    rows_ref[:edge] = jnp.zeros((edge, p), bf16)
    rows_ref[edge + R * s_count :] = jnp.zeros((edge, p), bf16)
    for k, slot in enumerate(slots(n_in)):
        ref, at = k_refs[min(k, n - 1)], max(k - (n - 1), 0)
        x = ref[at].T
        for e in range(g):
            i = (place_ref[1] ^ slot) * g + g - 1 - e
            to = pl.ds(pl.multiple_of(edge + i * s_count, s_count), s_count)
            rows_ref[to, :] = x[e * s_count : (e + 1) * s_count]
    wait()
    count = steps_of(lags)

    def block(b, _):
        def some(t, _):
            total = jnp.zeros(acc.shape, f32)
            for q in range(count):
                lag = t * count + q
                at = pl.ds(pl.multiple_of(lag * s_count, s_count), width)
                total += jnp.dot(
                    rows_ref[at, :], m_ref[b * g + lag], preferred_element_type=f32
                )

            @pl.when(t == 0)
            def _():
                acc[...] = total

            @pl.when(t > 0)
            def _():
                acc[...] += total

            return 0

        lax.fori_loop(0, lags // count, some, 0)
        for e in range(g):
            for d, o_ref in enumerate(o_refs):
                first = e * s_count + d * rows
                o_ref[b * g + g - 1 - e] = acc[first : first + rows].astype(o_ref.dtype)
        return 0

    lax.fori_loop(0, C // g, block, 0)


def corange_part(pieces, masked, place, n_out, n_in, before, whole):
    _, p, width = pieces[0].shape
    m = masked.shape[2]
    g = R // n_in
    s_count = width // g
    rows = s_count // n_out
    if whole:
        outs = [jax.ShapeDtypeStruct((n_out, C, rows, m), bf16)]
    else:
        outs = [jax.ShapeDtypeStruct((C, rows, m), bf16 if d else f32) for d in range(n_out)]
    return pl.pallas_call(
        functools.partial(corange_kernel, n_in, n_out, len(before)),
        in_specs=[pl.BlockSpec(memory_space=pltpu.SMEM)]
        + vmem_specs(pieces)
        + any_specs([masked, *before]),
        out_specs=vmem_specs(outs),
        out_shape=outs,
        scratch_shapes=[
            pltpu.VMEM((LAGS, p, m), bf16),
            pltpu.VMEM(((R + 2 * (g - 1)) * s_count, p), bf16),
            pltpu.VMEM((width, m), f32),
            pltpu.SemaphoreType.DMA((9,)),
        ],
        compiler_params=pltpu.CompilerParams(vmem_limit_bytes=VMEM),
        cost_estimate=product_cost(p, m, s_count if whole else 1),
        name="corange_part",
    )(place, *pieces, masked, *before)


def probe_order(z, n_out, width, s_count, e):
    rows = s_count // n_out
    shape = (PARTS * width, PARTS * s_count)
    come = lax.broadcasted_iota(jnp.int32, shape, 0)
    to = lax.broadcasted_iota(jnp.int32, shape, 1)
    q, col = come // width, come % width
    s = col % s_count
    place = (z + s // rows) % n_out * (PARTS * rows) + q * rows + s % rows
    return jnp.where((col // s_count == e) & (place == to), 1.0, 0.0).astype(bf16)


def gram_kernel(n_out, g, place_ref, *refs):
    k_refs, gram_ref = refs[:PARTS], refs[PARTS]
    width = k_refs[0].shape[2]
    x = jnp.concatenate([ref[0] for ref in k_refs], axis=1)
    total = jnp.zeros(gram_ref.shape, f32)
    for e in range(g):
        order = probe_order(place_ref[0], n_out, width, width // g, e)
        y = jnp.dot(x, order, preferred_element_type=f32).T.astype(bf16)
        total += lax.dot_general(y, y, (((1,), (1,)), ((), ())), preferred_element_type=f32)
    gram_ref[...] = total


def gram_part(own, place, n_out, g):
    s_count = PARTS * own[0].shape[2] // g
    return pl.pallas_call(
        functools.partial(gram_kernel, n_out, g),
        in_specs=[pl.BlockSpec(memory_space=pltpu.SMEM)] + vmem_specs(own),
        out_specs=pl.BlockSpec(memory_space=pltpu.VMEM),
        out_shape=jax.ShapeDtypeStruct((s_count, s_count), f32),
        name="gram_part",
    )(place, *own)


def finish_kernel(n_out, n_in, place_ref, *refs):
    o_ref, order = refs[-2:]
    n, g = n_in // 2 + 1, R // n_in
    width = refs[0].shape[2]
    for e in range(g):
        order[e] = probe_order(place_ref[0], n_out, width, width // g, e)
    for k, slot in enumerate(slots(n_in)):
        ref, at = min(k, n - 1), max(k - (n - 1), 0)
        x = jnp.concatenate([refs[q * n + ref][at] for q in range(PARTS)], axis=1)
        for e in range(g):
            y = jnp.dot(x, order[e], preferred_element_type=f32)
            o_ref[(place_ref[1] ^ slot) * g + g - 1 - e] = y.astype(bf16)


def finish(pieces, place, after, n_out, n_in):
    _, p, width = pieces[0][0].shape
    g = R // n_in
    flat = [x for part in pieces for x in part]
    return pl.pallas_call(
        functools.partial(finish_kernel, n_out, n_in),
        in_specs=[pl.BlockSpec(memory_space=pltpu.SMEM)] + vmem_specs(flat) + any_specs(after),
        out_specs=pl.BlockSpec(memory_space=pltpu.VMEM),
        out_shape=jax.ShapeDtypeStruct((R, p, PARTS * width // g), bf16),
        scratch_shapes=[pltpu.VMEM((g, PARTS * width, PARTS * width // g), bf16)],
        compiler_params=pltpu.CompilerParams(vmem_limit_bytes=VMEM),
        cost_estimate=pl.CostEstimate(flops=0, bytes_accessed=16 << 20, transcendentals=0),
        name="finish",
    )(place, *flat, *after)


def total_kernel(n, *refs):
    done, rest, o_ref = refs[:n], refs[n:-2], refs[-1]
    rows = rest[0].shape[1]
    total = rest[0][...]
    for ref in rest[1:]:
        total += ref[...].astype(f32)
    for q, x in enumerate([*[ref[...].astype(f32) for ref in done], total]):
        o_ref[q * rows : (q + 1) * rows] = jnp.swapaxes(x, 0, 1)


def total_corange(done, own, arrived, before):
    lags, rows, m = own.shape
    return pl.pallas_call(
        functools.partial(total_kernel, len(done)),
        in_specs=vmem_specs([*done, own, *arrived]) + any_specs([before]),
        out_specs=pl.BlockSpec(memory_space=pltpu.VMEM),
        out_shape=jax.ShapeDtypeStruct((rows * PARTS, lags, m), f32),
        name="total_corange",
    )(*done, own, *arrived, before)


def slots(n):
    return [*range(0, n, 2), *range(1, n, 2)]


def to_xor(x, axis, r, n):
    return lax.ppermute(x, axis, [(d, d ^ r) for d in range(n)])


def settle_kernel(n, keep_ref, away_ref, *refs):
    total = keep_ref[...] + away_ref[...].astype(f32)
    for ref in refs[:n]:
        total += ref[...].astype(f32)
    refs[-1][...] = total.astype(bf16)


def settle(keep, away, arrived, before):
    block = pl.BlockSpec((1, *keep.shape[1:]), lambda i: (0, 0, 0))
    return pl.pallas_call(
        functools.partial(settle_kernel, len(arrived)),
        grid=(1,),
        in_specs=[block] * (2 + len(arrived)) + any_specs(before),
        out_specs=block,
        out_shape=jax.ShapeDtypeStruct(arrived[0].shape, bf16),
        compiler_params=pltpu.CompilerParams(vmem_limit_bytes=VMEM),
        cost_estimate=pl.CostEstimate(
            flops=0, bytes_accessed=8 * arrived[0].size, transcendentals=0
        ),
        name="settle",
    )(keep, away, *arrived, *before)


def pair_kernel(keep_ref, away_ref, *refs):
    refs[-1][...] = (keep_ref[...] + away_ref[...].astype(f32)).astype(bf16)


def pair(keep, away, before):
    n, *rest = keep.shape
    block = pl.BlockSpec((1, *rest), lambda i: (i + 1, 0, 0))
    return pl.pallas_call(
        pair_kernel,
        grid=(n - 1,),
        in_specs=[block, block] + any_specs(before),
        out_specs=pl.BlockSpec((1, *rest), lambda i: (i, 0, 0)),
        out_shape=jax.ShapeDtypeStruct((n - 1, *rest), bf16),
        compiler_params=pltpu.CompilerParams(vmem_limit_bytes=VMEM),
        cost_estimate=pl.CostEstimate(flops=0, bytes_accessed=8 * keep.size, transcendentals=0),
        name="pair",
    )(keep, away, *before)


def spread(own, n):
    return [own] + [to_xor(own, "in", 2 * k, n) for k in range(1, n // 2)]


def join_kernel(n, *refs):
    rows = refs[0].shape[0]
    for k in range(n):
        refs[-1][k * rows : (k + 1) * rows] = refs[k][...]


def join(mine, before):
    rows, *rest = mine[0].shape
    return pl.pallas_call(
        functools.partial(join_kernel, len(mine)),
        in_specs=vmem_specs(mine) + any_specs(before),
        out_specs=pl.BlockSpec(memory_space=pltpu.VMEM),
        out_shape=jax.ShapeDtypeStruct((len(mine) * rows, *rest), bf16),
        name="join",
    )(*mine, *before)


def shards(n_out, n_in, markov, probes, pattern):
    rows = probes.shape[0] // PARTS
    z, idx = lax.axis_index("out"), lax.axis_index("in")
    place = jnp.stack([z, idx]).astype(jnp.int32)

    turned = jnp.swapaxes(probes, 0, 1)
    own = turned[:, :rows]
    gathered = [own]
    for d in range(1, n_out):
        gathered.append(lax.ppermute(own, "out", [((k + d) % n_out, k) for k in range(n_out)]))
    for q in range(1, PARTS):
        gathered.append(lax.all_gather(turned[:, q * rows : (q + 1) * rows], "out"))
    keeper = jnp.repeat(jnp.repeat(pattern, BO, axis=0), BI, axis=1).astype(bf16)
    masked = markov * keeper[None]

    parts = [gathered[:n_out]] + [[x] for x in gathered[n_out:]]
    raws = [sketch_part(u, masked, place, n_out, n_in) for u in parts]
    aways = [to_xor(send, "in", 1, n_in) for _, send in raws]
    leaving = [
        pair(raw[0], away, [raws[-1][1]] if q == 0 else [])
        for q, (raw, away) in enumerate(zip(raws, aways))
    ]
    met = []
    for (keep, _), away, x in zip(raws, aways, leaving):
        there = [to_xor(x[k - 1 : k], "in", 2 * k, n_in) for k in range(1, n_in // 2)]
        met.append((keep, away, there))

    owns, sums, summed, before = [], [], [], leaving[1:]
    for q, x in enumerate(met):
        owns.append(settle(*x, before))
        mine = spread(owns[q], n_in)
        last = q == PARTS - 1
        gram = [gram_part(owns, place, n_out, R // n_in)] if last else []
        if last:
            for bit in range(n_in.bit_length() - 1):
                gram = [gram[0] + to_xor(gram[0], "in", 1 << bit, n_in)]
        sums.append(mine + [to_xor(join(mine, gram), "in", 1, n_in)])
        cor = corange_part(sums[q], masked, place, n_out, n_in, before, not last)
        before = [cor[-1]]
        if not last:
            whole = cor[0].reshape((-1,) + cor[0].shape[2:])
            summed.append(lax.psum_scatter(whole, "out", scatter_dimension=0, tiled=True))

    (gram,) = gram
    for bit in range(n_out.bit_length() - 1):
        gram = gram + to_xor(gram, "out", 1 << bit, n_out)
    gram_matrix = gram / (R * OUTPUT_CHANNELS)

    arrived = [
        lax.ppermute(cor[d], "out", [(k, (k + d) % n_out) for k in range(n_out)])
        for d in range(1, n_out)
    ]
    sketch = finish(sums, place, [*summed, *before, gram_matrix], n_out, n_in)
    corange = total_corange(summed, cor[0], arrived, sketch)
    return (sketch, corange, gram_matrix)


def solution(mesh):
    body = functools.partial(shards, mesh.shape["out"], mesh.shape["in"])
    return jax.shard_map(
        body,
        mesh=mesh,
        in_specs=(P(None, "out", "in"), P("out", None, "in"), P("out", "in")),
        out_specs=(P(None, "out", None), P("out", None, "in"), P()),
        check_vma=False,
    )
```

```python
import functools

import jax
import jax.numpy as jnp
import ml_dtypes
import numpy as np
from jax import lax
from jax.experimental import pallas as pl
from jax.experimental.pallas import tpu as pltpu
from jax.sharding import PartitionSpec as P

OUTPUT_CHANNELS = 2048
BO = 64
BI = 128
R = 32
C = 32
LAGS = 63
F = 32
PARTS = 2
MARKOV_PARTS = 1
CHUNK = 4
VMEM = 60 << 20

bf16 = jnp.bfloat16
f32 = jnp.float32


def split(a):
    hi = a.astype(ml_dtypes.bfloat16)
    lo = (a - hi.astype(np.float64)).astype(ml_dtypes.bfloat16)
    return np.concatenate([hi, lo], axis=0)


def constants():
    theta = np.pi * (2 * np.arange(F)[:, None] + 1) / 64
    lag = np.arange(64)[None]
    cos, sin = np.cos(theta * lag), np.sin(theta * lag)
    eye = np.eye(8)
    fwd = np.stack([cos, sin])
    lag_mat = np.einsum("cfk,pq->cfpkq", fwd, eye).reshape(2 * F * 8, 64 * 8)
    half = fwd[:, :, :32]
    probe_mat = np.einsum("cfj,pq->cfpqj", half, eye).reshape(2 * F * 8, 32 * 8)
    sketch_mat = np.einsum("cfj,pq->cfpjq", half, eye).reshape(2 * F * 8, 32 * 8)
    back = half / F
    raw_mat = np.einsum("cfi,pq->ipcfq", back, eye).reshape(32 * 8, 2 * F * 8)
    cor_mat = np.einsum("cfj,pq->pjcfq", back, eye).reshape(32 * 8, 2 * F * 8)
    return [split(a) for a in (lag_mat, probe_mat, sketch_mat, raw_mat, cor_mat)]


def both(mat_ref, x):
    y = jnp.dot(mat_ref[...], x, preferred_element_type=f32)
    n = y.shape[0] // 2
    return y[:n] + y[n:]


def lag_kernel(keep_ref, mat_ref, x_ref, o_ref):
    rows, m = x_ref.shape[1], x_ref.shape[2]
    keep = keep_ref[0].astype(f32)

    def body(b, _):
        at = pl.ds(pl.multiple_of(b * 16, 16), 16)
        x = x_ref[:, at, :].astype(f32) * keep[None]
        res = []
        for h in range(2):
            part = x[:, 8 * h : 8 * h + 8, :].reshape(LAGS * 8, m)
            part = jnp.concatenate([part, jnp.zeros((8, m), f32)], axis=0)
            res.append(both(mat_ref, part.astype(bf16)).reshape(2, F, 8, m))
        y = jnp.concatenate(res, axis=2).astype(bf16)
        o_ref[:, at, 0:m] = y[0]
        o_ref[:, at, m : 2 * m] = y[1]
        return 0

    lax.fori_loop(0, rows // 16, body, 0)


def lag_transform(markov, keep, mat, part):
    lags, p, m = markov.shape
    blocks = p // BO // MARKOV_PARTS
    return pl.pallas_call(
        lag_kernel,
        grid=(blocks,),
        in_specs=[
            pl.BlockSpec((1, 1, m), lambda i: (part * blocks + i, 0, 0)),
            pl.BlockSpec(mat.shape, lambda i: (0, 0)),
            pl.BlockSpec((lags, BO, m), lambda i: (0, part * blocks + i, 0)),
        ],
        out_specs=pl.BlockSpec((F, BO, 2 * m), lambda i: (0, i, 0)),
        out_shape=jax.ShapeDtypeStruct((F, p // MARKOV_PARTS, 2 * m), bf16),
        compiler_params=pltpu.CompilerParams(vmem_limit_bytes=VMEM),
        cost_estimate=pl.CostEstimate(
            flops=p * m * 1024 * 64, bytes_accessed=2 * 64 * p * m, transcendentals=0
        ),
        name="lag_transform",
    )(keep, mat, markov)


def rotate_into(hat_ref, y, at, at2, lo, hi):
    c, s = y[0].astype(bf16), y[1].astype(bf16)
    hat_ref[:, at, lo] = c
    hat_ref[:, at2, hi] = c
    hat_ref[:, at, hi] = s
    hat_ref[:, at2, lo] = -s


def fetch(m_hbms, m_ref, sems):
    rows = m_ref.shape[1] // MARKOV_PARTS

    def copies(c):
        at = pl.ds(c * CHUNK, CHUNK)
        return [
            pltpu.make_async_copy(
                m_hbm.at[at], m_ref.at[at, pl.ds(k * rows, rows)], sems.at[k, c]
            )
            for k, m_hbm in enumerate(m_hbms)
        ]

    for c in range(F // CHUNK):
        for copy in copies(c):
            copy.start()
    return copies


def over_frequencies(copies, one):
    def body(c, _):
        for copy in copies(c):
            copy.wait()
        for k in range(CHUNK):
            one(c * CHUNK + k)
        return 0

    lax.fori_loop(0, F // CHUNK, body, 0)


def back_input(freq, b, h, s_count, cols):
    re = freq[:, pl.ds(pl.multiple_of(b * 16 + 8 * h, 8), 8), cols]
    im = freq[:, pl.ds(pl.multiple_of(s_count + b * 16 + 8 * h, 8), 8), cols]
    x = jnp.concatenate([re, im], axis=0)
    return x.reshape(2 * F * 8, x.shape[-1]).astype(bf16)


def sketch_kernel(n, n_out, n_in, place_ref, fwd_ref, back_ref, *refs):
    u_refs, m_hbms, refs = refs[:n], refs[n : n + MARKOV_PARTS], refs[n + MARKOV_PARTS :]
    sums, (back, m_ref, hat, freq, sems) = refs[: 2 * PARTS], refs[2 * PARTS :]
    whole = u_refs[n_out:]
    u_refs = list(u_refs[:n_out])
    for ref in whole:
        u_refs += [ref.at[lax.rem(place_ref[0] + d, n_out)] for d in range(n_out)]
    rows, _, m = u_refs[0].shape
    s_count, p = n_out * PARTS * rows, m_ref.shape[1]
    copies = fetch(m_hbms, m_ref, sems)

    for b in range(s_count // 16):
        res = []
        for g in (2 * b, 2 * b + 1):
            first = (g * 8) % rows
            x = u_refs[g * 8 // rows][first : first + 8].reshape(8 * C, m)
            res.append(both(fwd_ref, x).reshape(2, F, 8, m))
        y = jnp.concatenate(res, axis=2)
        at, at2 = pl.ds(b * 16, 16), pl.ds(s_count + b * 16, 16)
        rotate_into(hat, y, at, at2, slice(0, m), slice(m, 2 * m))

    def one(f):
        freq[f] = lax.dot_general(
            hat[f], m_ref[f], (((1,), (1,)), ((), ())), preferred_element_type=f32
        )

    over_frequencies(copies, one)
    width = min(p, 256)
    g = R // n_in * 8
    for part in range(2):
        for k, slot in enumerate(slots(n_in)):
            at = pl.ds(pl.multiple_of(part * R * 8 + (place_ref[1] ^ slot) * g, 16), g)
            back[part * R * 8 + k * g : part * R * 8 + (k + 1) * g] = back_ref[at]

    for q in range(PARTS):
        keep_ref, send_ref = sums[2 * q : 2 * q + 2]
        part = s_count // PARTS // 16

        def body(b, _):
            at = pl.ds(pl.multiple_of(b * 16, 16), 16)
            for w in range(p // width):
                cols = slice(w * width, (w + 1) * width)
                res = []
                for h in range(2):
                    x = back_input(freq, q * part + b, h, s_count, cols)
                    res.append(both(back, x).reshape(R, 8, width))
                y = jnp.concatenate(res, axis=1)
                keep_ref[:, at, cols] = y[: R // 2]
                send_ref[:, at, cols] = y[R // 2 :].astype(bf16)
            return 0

        lax.fori_loop(0, part, body, 0)


def vmem_specs(arrays):
    return [pl.BlockSpec(memory_space=pltpu.VMEM) for _ in arrays]


def any_specs(arrays):
    return [pl.BlockSpec(memory_space=pl.ANY) for _ in arrays]


NO_COST = pl.CostEstimate(flops=0, bytes_accessed=1, transcendentals=0)


def product_cost(p, m, extra):
    return pl.CostEstimate(
        flops=2 * F * 256 * 2 * m * p * 2, bytes_accessed=4 * F * p * m + extra, transcendentals=0
    )


def sketch_part(probes, hankel, fwd, back, place, n_out, n_in):
    rows, _, m = probes[0].shape
    p = hankel[0].shape[1] * MARKOV_PARTS
    part, s_count = rows * n_out, rows * n_out * PARTS
    return pl.pallas_call(
        functools.partial(sketch_kernel, len(probes), n_out, n_in),
        in_specs=[pl.BlockSpec(memory_space=pltpu.SMEM)]
        + vmem_specs([fwd, back, *probes])
        + any_specs(hankel),
        out_specs=vmem_specs(range(2 * PARTS)),
        out_shape=[
            jax.ShapeDtypeStruct((R // 2, part, p), f32),
            jax.ShapeDtypeStruct((R // 2, part, p), bf16),
        ]
        * PARTS,
        scratch_shapes=[
            pltpu.VMEM(back.shape, bf16),
            pltpu.VMEM((F, p, 2 * m), bf16),
            pltpu.VMEM((F, 2 * s_count, 2 * m), bf16),
            pltpu.VMEM((F, 2 * s_count, p), f32),
            pltpu.SemaphoreType.DMA((MARKOV_PARTS, F // CHUNK)),
        ],
        compiler_params=pltpu.CompilerParams(vmem_limit_bytes=VMEM),
        cost_estimate=product_cost(p, m, 0),
        name="sketch_part",
    )(place, fwd, back, *probes, *hankel)


def corange_kernel(n_in, n_out, n_before, n_o, place_ref, fwd_ref, back_ref, *refs):
    k_refs, refs = refs[: n_in // 2 + 1], refs[n_in // 2 + 1 :]
    m_hbms, refs = refs[:MARKOV_PARTS], refs[MARKOV_PARTS + n_before :]
    o_refs, (fwd, m_ref, hat, freq, sems) = refs[:n_o], refs[n_o:]
    if n_o == 1:
        o_refs = [o_refs[0].at[lax.rem(place_ref[0] + d, n_out)] for d in range(n_out)]
    _, s_count, p = k_refs[0].shape
    m = m_ref.shape[2] // 2
    rows = s_count // n_out
    copies = fetch(m_hbms, m_ref, sems)
    width = min(p, 256)

    g = R // n_in * 8
    to = lax.broadcasted_iota(jnp.int32, (R * 8, R * 8), 1)
    come = lax.broadcasted_iota(jnp.int32, (R * 8, R * 8), 0)
    where = to // g
    slot = jnp.where(where < n_in // 2, 2 * where, 2 * where - (n_in - 1))
    moved = come == (place_ref[1] ^ slot) * g + to % g
    move = jnp.where(moved, 1.0, 0.0).astype(bf16)
    fwd[...] = jnp.dot(fwd_ref[...], move, preferred_element_type=f32).astype(bf16)

    def forward(b, _):
        at = pl.ds(pl.multiple_of(b * 16, 16), 16)
        at2 = pl.ds(pl.multiple_of(s_count + b * 16, 16), 16)
        for w in range(p // width):
            cols = slice(w * width, (w + 1) * width)
            k = jnp.concatenate([ref[:, at, cols] for ref in k_refs], axis=0).astype(f32)
            res = []
            for h in range(2):
                x = k[:, 8 * h : 8 * h + 8, :].reshape(R * 8, width).astype(bf16)
                res.append(both(fwd, x).reshape(2, F, 8, width))
            y = jnp.concatenate(res, axis=2)
            lo = slice(w * width, (w + 1) * width)
            hi = slice(p + w * width, p + (w + 1) * width)
            rotate_into(hat, y, at, at2, lo, hi)
        return 0

    lax.fori_loop(0, s_count // 16, forward, 0)

    def one(f):
        left = hat[f]
        freq[f] = jnp.dot(left[:, :p], m_ref[f, :, :m], preferred_element_type=f32) + jnp.dot(
            left[:, p:], m_ref[f, :, m:], preferred_element_type=f32
        )

    over_frequencies(copies, one)

    for g in range(s_count // 8):
        x = back_input(freq, g // 2, g % 2, s_count, slice(0, m))
        first = (g * 8) % rows
        o_ref = o_refs[g * 8 // rows]
        o_ref[first : first + 8] = both(back_ref, x).reshape(8, C, m).astype(o_ref.dtype)


def corange_part(pieces, hankel, fwd, back, place, n_out, n_in, before, whole):
    _, s_count, p = pieces[0].shape
    m = hankel[0].shape[2] // 2
    rows = s_count // n_out
    if whole:
        outs = [jax.ShapeDtypeStruct((n_out, rows, C, m), bf16)]
    else:
        outs = [jax.ShapeDtypeStruct((rows, C, m), bf16 if d else f32) for d in range(n_out)]
    return pl.pallas_call(
        functools.partial(corange_kernel, n_in, n_out, len(before), len(outs)),
        in_specs=[pl.BlockSpec(memory_space=pltpu.SMEM)]
        + vmem_specs([fwd, back, *pieces])
        + any_specs([*hankel, *before]),
        out_specs=vmem_specs(outs),
        out_shape=outs,
        scratch_shapes=[
            pltpu.VMEM(fwd.shape, bf16),
            pltpu.VMEM((F, p, 2 * m), bf16),
            pltpu.VMEM((F, 2 * s_count, 2 * p), bf16),
            pltpu.VMEM((F, 2 * s_count, m), f32),
            pltpu.SemaphoreType.DMA((MARKOV_PARTS, F // CHUNK)),
        ],
        compiler_params=pltpu.CompilerParams(vmem_limit_bytes=VMEM),
        cost_estimate=product_cost(p, m, 0) if whole else NO_COST,
        name="corange_part",
    )(place, fwd, back, *pieces, *hankel, *before)


def in_order(x, both_parts, q, z, n_out):
    rows = x.shape[0] // n_out
    x = x.astype(f32)
    for d in range(n_out):
        first = lax.rem(z + d, n_out) * (PARTS * rows) + q * rows
        both_parts[pl.ds(pl.multiple_of(first, 8), rows), :] = x[d * rows : (d + 1) * rows]


def gram_kernel(n_out, place_ref, *refs):
    k_refs, (gram_ref, both_parts) = refs[:PARTS], refs[PARTS:]
    gram_ref[...] = jnp.zeros(gram_ref.shape, f32)

    def body(i, _):
        for q, ref in enumerate(k_refs):
            in_order(ref[i], both_parts, q, place_ref[0], n_out)
        x = both_parts[...].astype(bf16)
        gram_ref[...] += lax.dot_general(
            x, x, (((1,), (1,)), ((), ())), preferred_element_type=f32
        )
        return 0

    lax.fori_loop(0, k_refs[0].shape[0], body, 0)


def gram_part(joined, place, n_out):
    _, s_count, p = joined[0].shape
    s_count *= PARTS
    return pl.pallas_call(
        functools.partial(gram_kernel, n_out),
        in_specs=[pl.BlockSpec(memory_space=pltpu.SMEM)] + vmem_specs(joined),
        out_specs=pl.BlockSpec(memory_space=pltpu.VMEM),
        out_shape=jax.ShapeDtypeStruct((s_count, s_count), f32),
        scratch_shapes=[pltpu.VMEM((s_count, p), f32)],
        compiler_params=pltpu.CompilerParams(vmem_limit_bytes=VMEM),
        name="gram_part",
    )(place, *joined)


def total_kernel(n, *refs):
    done, rest, o_ref = refs[:n], refs[n:-2], refs[-1]
    rows = rest[0].shape[0]
    for q, ref in enumerate(done):
        o_ref[q * rows : (q + 1) * rows] = ref[...].astype(f32)
    total = rest[0][...]
    for ref in rest[1:]:
        total += ref[...].astype(f32)
    o_ref[n * rows :] = total


def total_corange(done, own, arrived, before):
    rows, *rest = own.shape
    return pl.pallas_call(
        functools.partial(total_kernel, len(done)),
        in_specs=vmem_specs([*done, own, *arrived]) + any_specs([before]),
        out_specs=pl.BlockSpec(memory_space=pltpu.VMEM),
        out_shape=jax.ShapeDtypeStruct((rows * PARTS, *rest), f32),
        name="total_corange",
    )(*done, own, *arrived, before)


def finish_kernel(n_out, n_in, place_ref, *refs):
    o_ref, both_parts = refs[-2:]
    n = n_in // 2 + 1
    i_count = refs[0].shape[0]
    z, idx = place_ref[0], place_ref[1]
    for k, slot in enumerate(slots(n_in)):
        ref, base = min(k, n - 1), max(k - (n - 1), 0) * i_count

        def body(t, _):
            for q in range(PARTS):
                in_order(refs[q * n + ref][base + t], both_parts, q, z, n_out)
            o_ref[(idx ^ slot) * i_count + t] = both_parts[...].T.astype(bf16)
            return 0

        lax.fori_loop(0, i_count, body, 0)


def finish(pieces, place, after, n_out, n_in):
    i_count, s_count, p = pieces[0][0].shape
    flat = [x for part in pieces for x in part]
    return pl.pallas_call(
        functools.partial(finish_kernel, n_out, n_in),
        in_specs=[pl.BlockSpec(memory_space=pltpu.SMEM)] + vmem_specs(flat) + any_specs(after),
        out_specs=pl.BlockSpec(memory_space=pltpu.VMEM),
        out_shape=jax.ShapeDtypeStruct((R, p, PARTS * s_count), bf16),
        scratch_shapes=[pltpu.VMEM((PARTS * s_count, p), f32)],
        compiler_params=pltpu.CompilerParams(vmem_limit_bytes=VMEM),
        cost_estimate=pl.CostEstimate(
            flops=0, bytes_accessed=64 * R * p * s_count, transcendentals=0
        ),
        name="finish",
    )(place, *flat, *after)


def slots(n):
    return [*range(0, n, 2), *range(1, n, 2)]


def to_xor(x, axis, r, n):
    return lax.ppermute(x, axis, [(d, d ^ r) for d in range(n)])


def sum_by_xor(x, axis, n):
    step = 1
    while step < n:
        if 4 * step <= n:
            a, b, c = [to_xor(x, axis, k * step, n) for k in (1, 2, 3)]
            x = (x + a) + (b + c)
            step *= 4
        else:
            x = x + to_xor(x, axis, step, n)
            step *= 2
    return x


def settle_kernel(n, keep_ref, away_ref, *refs):
    total = keep_ref[...] + away_ref[...].astype(f32)
    for ref in refs[:n]:
        total += ref[...].astype(f32)
    refs[-1][...] = total.astype(bf16)


def settle(keep, away, arrived, before):
    block = pl.BlockSpec(arrived[0].shape, lambda i: (0, 0, 0))
    return pl.pallas_call(
        functools.partial(settle_kernel, len(arrived)),
        grid=(1,),
        in_specs=[block] * (2 + len(arrived)) + any_specs(before),
        out_specs=block,
        out_shape=jax.ShapeDtypeStruct(arrived[0].shape, bf16),
        compiler_params=pltpu.CompilerParams(vmem_limit_bytes=VMEM),
        cost_estimate=pl.CostEstimate(
            flops=0, bytes_accessed=8 * arrived[0].size, transcendentals=0
        ),
        name="settle",
    )(keep, away, *arrived, *before)


def meet(keep, send, n):
    away = to_xor(send, "in", 1, n)
    g = R // n
    arrived = []
    for k in range(1, n // 2):
        rows = slice(k * g, (k + 1) * g)
        arrived.append(to_xor((keep[rows] + away[rows].astype(f32)).astype(bf16), "in", 2 * k, n))
    return keep, away, arrived


def spread(own, n):
    return [own] + [to_xor(own, "in", 2 * k, n) for k in range(1, n // 2)]


def join_kernel(n, *refs):
    rows = refs[0].shape[0]
    for k in range(n):
        refs[-1][k * rows : (k + 1) * rows] = refs[k][...]


def join(mine, before):
    rows, *rest = mine[0].shape
    return pl.pallas_call(
        functools.partial(join_kernel, len(mine)),
        in_specs=vmem_specs(mine) + any_specs(before),
        out_specs=pl.BlockSpec(memory_space=pltpu.VMEM),
        out_shape=jax.ShapeDtypeStruct((len(mine) * rows, *rest), bf16),
        name="join",
    )(*mine, *before)


def shards(n_out, n_in, mats, markov, probes, pattern):
    lag_mat, probe_mat, sketch_mat, raw_mat, cor_mat = [jnp.asarray(a) for a in mats]
    rows = probes.shape[0] // PARTS
    z, idx = lax.axis_index("out"), lax.axis_index("in")

    place = jnp.stack([z, idx]).astype(jnp.int32)
    keep = jnp.repeat(pattern, BI, axis=1).astype(f32)[:, None, :]

    own = probes[:rows]
    gathered = [own]
    for d in range(1, n_out):
        gathered.append(lax.ppermute(own, "out", [((k + d) % n_out, k) for k in range(n_out)]))
    for q in range(1, PARTS):
        gathered.append(lax.all_gather(probes[q * rows : (q + 1) * rows], "out"))
    hankel = [lag_transform(markov, keep, lag_mat, q) for q in range(MARKOV_PARTS)]

    raws = sketch_part(gathered, hankel, probe_mat, raw_mat, place, n_out, n_in)
    met = [meet(raws[2 * q], raws[2 * q + 1], n_in) for q in range(PARTS)]
    owns = [settle(*x, []) for x in met]
    joined, sums, summed, before = [], [], [], owns[-1:]
    for q, own in enumerate(owns):
        mine = spread(own, n_in)
        joined.append(join(mine, before if q else []))
        sums.append(mine + [to_xor(joined[q], "in", 1, n_in)])
        last = q == PARTS - 1
        cor = corange_part(
            sums[q], hankel, sketch_mat, cor_mat, place, n_out, n_in, before, not last
        )
        before = [cor[-1]]
        if not last:
            whole = cor[0].reshape((-1,) + cor[0].shape[2:])
            summed.append(lax.psum_scatter(whole, "out", scatter_dimension=0, tiled=True))

    arrived = [
        lax.ppermute(cor[d], "out", [(k, (k + d) % n_out) for k in range(n_out)])
        for d in range(1, n_out)
    ]
    gram = gram_part(joined, place, n_out)
    gram = sum_by_xor(gram + to_xor(gram, "in", 1, n_in), "out", n_out)
    gram_matrix = gram / (R * OUTPUT_CHANNELS)
    sketch = finish(sums, place, [*summed, *before, gram_matrix], n_out, n_in)
    corange = total_corange(summed, cor[0], arrived, sketch)
    return (sketch, corange, gram_matrix)


def solution(mesh):
    body = functools.partial(shards, mesh.shape["out"], mesh.shape["in"], constants())
    return jax.shard_map(
        body,
        mesh=mesh,
        in_specs=(P(None, "out", "in"), P("out", None, "in"), P("out", "in")),
        out_specs=(P(None, "out", None), P("out", None, "in"), P()),
        check_vma=False,
    )
```

```python
import functools

import jax
import jax.numpy as jnp
import ml_dtypes
import numpy as np
from jax import lax
from jax.experimental import pallas as pl
from jax.experimental.pallas import tpu as pltpu
from jax.sharding import PartitionSpec as P

OUTPUT_CHANNELS = 2048
BO = 64
BI = 128
R = 32
C = 32
LAGS = 63
F = 32
PARTS = 2
MARKOV_PARTS = 1
CHUNK = 4
VMEM = 60 << 20

bf16 = jnp.bfloat16
f32 = jnp.float32


def split(a):
    hi = a.astype(ml_dtypes.bfloat16)
    lo = (a - hi.astype(np.float64)).astype(ml_dtypes.bfloat16)
    return np.concatenate([hi, lo], axis=0)


def constants():
    theta = np.pi * (2 * np.arange(F)[:, None] + 1) / 64
    lag = np.arange(64)[None]
    cos, sin = np.cos(theta * lag), np.sin(theta * lag)
    eye = np.eye(8)
    fwd = np.stack([cos, sin])
    lag_mat = np.einsum("cfk,pq->cfpkq", fwd, eye).reshape(2 * F * 8, 64 * 8)
    half = fwd[:, :, :32]
    probe_mat = np.einsum("cfj,pq->cfpqj", half, eye).reshape(2 * F * 8, 32 * 8)
    sketch_mat = np.einsum("cfj,pq->cfpjq", half, eye).reshape(2 * F * 8, 32 * 8)
    back = half / F
    raw_mat = np.einsum("cfi,pq->ipcfq", back, eye).reshape(32 * 8, 2 * F * 8)
    cor_mat = np.einsum("cfj,pq->pjcfq", back, eye).reshape(32 * 8, 2 * F * 8)
    return [split(a) for a in (lag_mat, probe_mat, sketch_mat, raw_mat, cor_mat)]


def both(mat_ref, x):
    y = jnp.dot(mat_ref[...], x, preferred_element_type=f32)
    n = y.shape[0] // 2
    return y[:n] + y[n:]


def lag_kernel(keep_ref, mat_ref, x_ref, o_ref):
    rows, m = x_ref.shape[1], x_ref.shape[2]
    keep = keep_ref[0].astype(f32)

    def body(b, _):
        at = pl.ds(pl.multiple_of(b * 16, 16), 16)
        x = x_ref[:, at, :].astype(f32) * keep[None]
        res = []
        for h in range(2):
            part = x[:, 8 * h : 8 * h + 8, :].reshape(LAGS * 8, m)
            part = jnp.concatenate([part, jnp.zeros((8, m), f32)], axis=0)
            res.append(both(mat_ref, part.astype(bf16)).reshape(2, F, 8, m))
        y = jnp.concatenate(res, axis=2).astype(bf16)
        o_ref[:, at, 0:m] = y[0]
        o_ref[:, at, m : 2 * m] = y[1]
        return 0

    lax.fori_loop(0, rows // 16, body, 0)


def lag_transform(markov, keep, mat, part):
    lags, p, m = markov.shape
    blocks = p // BO // MARKOV_PARTS
    return pl.pallas_call(
        lag_kernel,
        grid=(blocks,),
        in_specs=[
            pl.BlockSpec((1, 1, m), lambda i: (part * blocks + i, 0, 0)),
            pl.BlockSpec(mat.shape, lambda i: (0, 0)),
            pl.BlockSpec((lags, BO, m), lambda i: (0, part * blocks + i, 0)),
        ],
        out_specs=pl.BlockSpec((F, BO, 2 * m), lambda i: (0, i, 0)),
        out_shape=jax.ShapeDtypeStruct((F, p // MARKOV_PARTS, 2 * m), bf16),
        compiler_params=pltpu.CompilerParams(vmem_limit_bytes=VMEM),
        cost_estimate=pl.CostEstimate(
            flops=p * m * 1024 * 64, bytes_accessed=2 * 64 * p * m, transcendentals=0
        ),
        name="lag_transform",
    )(keep, mat, markov)


def rotate_into(hat_ref, y, at, at2, lo, hi):
    c, s = y[0].astype(bf16), y[1].astype(bf16)
    hat_ref[:, at, lo] = c
    hat_ref[:, at2, hi] = c
    hat_ref[:, at, hi] = s
    hat_ref[:, at2, lo] = -s


def fetch(m_hbms, m_ref, sems):
    rows = m_ref.shape[1] // MARKOV_PARTS

    def copies(c):
        at = pl.ds(c * CHUNK, CHUNK)
        return [
            pltpu.make_async_copy(
                m_hbm.at[at], m_ref.at[at, pl.ds(k * rows, rows)], sems.at[k, c]
            )
            for k, m_hbm in enumerate(m_hbms)
        ]

    for c in range(F // CHUNK):
        for copy in copies(c):
            copy.start()
    return copies


def over_frequencies(copies, one):
    def body(c, _):
        for copy in copies(c):
            copy.wait()
        for k in range(CHUNK):
            one(c * CHUNK + k)
        return 0

    lax.fori_loop(0, F // CHUNK, body, 0)


def back_input(freq, b, h, s_count, cols):
    re = freq[:, pl.ds(pl.multiple_of(b * 16 + 8 * h, 8), 8), cols]
    im = freq[:, pl.ds(pl.multiple_of(s_count + b * 16 + 8 * h, 8), 8), cols]
    x = jnp.concatenate([re, im], axis=0)
    return x.reshape(2 * F * 8, x.shape[-1]).astype(bf16)


def sketch_kernel(n, n_out, n_in, place_ref, fwd_ref, back_ref, *refs):
    u_refs, m_hbms, refs = refs[:n], refs[n : n + MARKOV_PARTS], refs[n + MARKOV_PARTS :]
    sums, (back, m_ref, hat, freq, sems) = refs[: 2 * PARTS], refs[2 * PARTS :]
    whole = u_refs[n_out:]
    u_refs = list(u_refs[:n_out])
    for ref in whole:
        u_refs += [ref.at[lax.rem(place_ref[0] + d, n_out)] for d in range(n_out)]
    rows, _, m = u_refs[0].shape
    s_count, p = n_out * PARTS * rows, m_ref.shape[1]
    copies = fetch(m_hbms, m_ref, sems)

    for b in range(s_count // 16):
        res = []
        for g in (2 * b, 2 * b + 1):
            first = (g * 8) % rows
            x = u_refs[g * 8 // rows][first : first + 8].reshape(8 * C, m)
            res.append(both(fwd_ref, x).reshape(2, F, 8, m))
        y = jnp.concatenate(res, axis=2)
        at, at2 = pl.ds(b * 16, 16), pl.ds(s_count + b * 16, 16)
        rotate_into(hat, y, at, at2, slice(0, m), slice(m, 2 * m))

    def one(f):
        freq[f] = lax.dot_general(
            hat[f], m_ref[f], (((1,), (1,)), ((), ())), preferred_element_type=f32
        )

    over_frequencies(copies, one)
    width = min(p, 256)
    g = R // n_in * 8
    for part in range(2):
        for k, slot in enumerate(slots(n_in)):
            at = pl.ds(pl.multiple_of(part * R * 8 + (place_ref[1] ^ slot) * g, 16), g)
            back[part * R * 8 + k * g : part * R * 8 + (k + 1) * g] = back_ref[at]

    for q in range(PARTS):
        keep_ref, send_ref = sums[2 * q : 2 * q + 2]
        part = s_count // PARTS // 16

        def body(b, _):
            at = pl.ds(pl.multiple_of(b * 16, 16), 16)
            for w in range(p // width):
                cols = slice(w * width, (w + 1) * width)
                res = []
                for h in range(2):
                    x = back_input(freq, q * part + b, h, s_count, cols)
                    res.append(both(back, x).reshape(R, 8, width))
                y = jnp.concatenate(res, axis=1)
                keep_ref[:, at, cols] = y[: R // 2]
                send_ref[:, at, cols] = y[R // 2 :].astype(bf16)
            return 0

        lax.fori_loop(0, part, body, 0)


def vmem_specs(arrays):
    return [pl.BlockSpec(memory_space=pltpu.VMEM) for _ in arrays]


def any_specs(arrays):
    return [pl.BlockSpec(memory_space=pl.ANY) for _ in arrays]


def product_cost(p, m, extra):
    return pl.CostEstimate(
        flops=2 * F * 256 * 2 * m * p * 2, bytes_accessed=4 * F * p * m + extra, transcendentals=0
    )


def sketch_part(probes, hankel, fwd, back, place, n_out, n_in):
    rows, _, m = probes[0].shape
    p = hankel[0].shape[1] * MARKOV_PARTS
    part, s_count = rows * n_out, rows * n_out * PARTS
    return pl.pallas_call(
        functools.partial(sketch_kernel, len(probes), n_out, n_in),
        in_specs=[pl.BlockSpec(memory_space=pltpu.SMEM)]
        + vmem_specs([fwd, back, *probes])
        + any_specs(hankel),
        out_specs=vmem_specs(range(2 * PARTS)),
        out_shape=[
            jax.ShapeDtypeStruct((R // 2, part, p), f32),
            jax.ShapeDtypeStruct((R // 2, part, p), bf16),
        ]
        * PARTS,
        scratch_shapes=[
            pltpu.VMEM(back.shape, bf16),
            pltpu.VMEM((F, p, 2 * m), bf16),
            pltpu.VMEM((F, 2 * s_count, 2 * m), bf16),
            pltpu.VMEM((F, 2 * s_count, p), f32),
            pltpu.SemaphoreType.DMA((MARKOV_PARTS, F // CHUNK)),
        ],
        compiler_params=pltpu.CompilerParams(vmem_limit_bytes=VMEM),
        cost_estimate=product_cost(p, m, 0),
        name="sketch_part",
    )(place, fwd, back, *probes, *hankel)


def corange_kernel(n_in, n_out, n_before, n_o, place_ref, fwd_ref, back_ref, *refs):
    k_refs, refs = refs[: n_in // 2 + 1], refs[n_in // 2 + 1 :]
    m_hbms, refs = refs[:MARKOV_PARTS], refs[MARKOV_PARTS + n_before :]
    o_refs, (fwd, m_ref, hat, freq, sems) = refs[:n_o], refs[n_o:]
    if n_o == 1:
        o_refs = [o_refs[0].at[lax.rem(place_ref[0] + d, n_out)] for d in range(n_out)]
    _, s_count, p = k_refs[0].shape
    m = m_ref.shape[2] // 2
    rows = s_count // n_out
    copies = fetch(m_hbms, m_ref, sems)
    width = min(p, 256)

    g = R // n_in * 8
    to = lax.broadcasted_iota(jnp.int32, (R * 8, R * 8), 1)
    come = lax.broadcasted_iota(jnp.int32, (R * 8, R * 8), 0)
    where = to // g
    slot = jnp.where(where < n_in // 2, 2 * where, 2 * where - (n_in - 1))
    moved = come == (place_ref[1] ^ slot) * g + to % g
    move = jnp.where(moved, 1.0, 0.0).astype(bf16)
    fwd[...] = jnp.dot(fwd_ref[...], move, preferred_element_type=f32).astype(bf16)

    def forward(b, _):
        at = pl.ds(pl.multiple_of(b * 16, 16), 16)
        at2 = pl.ds(pl.multiple_of(s_count + b * 16, 16), 16)
        for w in range(p // width):
            cols = slice(w * width, (w + 1) * width)
            k = jnp.concatenate([ref[:, at, cols] for ref in k_refs], axis=0).astype(f32)
            res = []
            for h in range(2):
                x = k[:, 8 * h : 8 * h + 8, :].reshape(R * 8, width).astype(bf16)
                res.append(both(fwd, x).reshape(2, F, 8, width))
            y = jnp.concatenate(res, axis=2)
            lo = slice(w * width, (w + 1) * width)
            hi = slice(p + w * width, p + (w + 1) * width)
            rotate_into(hat, y, at, at2, lo, hi)
        return 0

    lax.fori_loop(0, s_count // 16, forward, 0)

    def one(f):
        left = hat[f]
        freq[f] = jnp.dot(left[:, :p], m_ref[f, :, :m], preferred_element_type=f32) + jnp.dot(
            left[:, p:], m_ref[f, :, m:], preferred_element_type=f32
        )

    over_frequencies(copies, one)

    for g in range(s_count // 8):
        x = back_input(freq, g // 2, g % 2, s_count, slice(0, m))
        first = (g * 8) % rows
        o_ref = o_refs[g * 8 // rows]
        o_ref[first : first + 8] = both(back_ref, x).reshape(8, C, m).astype(o_ref.dtype)


def corange_part(pieces, hankel, fwd, back, place, n_out, n_in, before, whole):
    _, s_count, p = pieces[0].shape
    m = hankel[0].shape[2] // 2
    rows = s_count // n_out
    if whole:
        outs = [jax.ShapeDtypeStruct((n_out, rows, C, m), bf16)]
    else:
        outs = [jax.ShapeDtypeStruct((rows, C, m), bf16 if d else f32) for d in range(n_out)]
    return pl.pallas_call(
        functools.partial(corange_kernel, n_in, n_out, len(before), len(outs)),
        in_specs=[pl.BlockSpec(memory_space=pltpu.SMEM)]
        + vmem_specs([fwd, back, *pieces])
        + any_specs([*hankel, *before]),
        out_specs=vmem_specs(outs),
        out_shape=outs,
        scratch_shapes=[
            pltpu.VMEM(fwd.shape, bf16),
            pltpu.VMEM((F, p, 2 * m), bf16),
            pltpu.VMEM((F, 2 * s_count, 2 * p), bf16),
            pltpu.VMEM((F, 2 * s_count, m), f32),
            pltpu.SemaphoreType.DMA((MARKOV_PARTS, F // CHUNK)),
        ],
        compiler_params=pltpu.CompilerParams(vmem_limit_bytes=VMEM),
        cost_estimate=product_cost(p, m, 0),
        name="corange_part",
    )(place, fwd, back, *pieces, *hankel, *before)


def in_order(x, both_parts, q, z, n_out):
    rows = x.shape[0] // n_out
    x = x.astype(f32)
    for d in range(n_out):
        first = lax.rem(z + d, n_out) * (PARTS * rows) + q * rows
        both_parts[pl.ds(pl.multiple_of(first, 8), rows), :] = x[d * rows : (d + 1) * rows]


def gram_kernel(n_out, place_ref, *refs):
    k_refs, (gram_ref, moved) = refs[:PARTS], refs[PARTS:]
    s_count = k_refs[0].shape[1]
    total = jnp.zeros(gram_ref.shape, f32)
    for i in range(k_refs[0].shape[0]):
        x = jnp.concatenate([ref[i] for ref in k_refs], axis=0)
        total += lax.dot_general(x, x, (((1,), (1,)), ((), ())), preferred_element_type=f32)
    for _ in range(2):
        for q in range(PARTS):
            in_order(total[q * s_count : (q + 1) * s_count], moved, q, place_ref[0], n_out)
        total = moved[...].T
    gram_ref[...] = total


def gram_part(joined, place, n_out):
    s_count = PARTS * joined[0].shape[1]
    return pl.pallas_call(
        functools.partial(gram_kernel, n_out),
        in_specs=[pl.BlockSpec(memory_space=pltpu.SMEM)] + vmem_specs(joined),
        out_specs=pl.BlockSpec(memory_space=pltpu.VMEM),
        out_shape=jax.ShapeDtypeStruct((s_count, s_count), f32),
        scratch_shapes=[pltpu.VMEM((s_count, s_count), f32)],
        compiler_params=pltpu.CompilerParams(vmem_limit_bytes=VMEM),
        name="gram_part",
    )(place, *joined)


def total_kernel(n, *refs):
    done, rest, o_ref = refs[:n], refs[n:-2], refs[-1]
    rows = rest[0].shape[0]
    for q, ref in enumerate(done):
        o_ref[q * rows : (q + 1) * rows] = ref[...].astype(f32)
    total = rest[0][...]
    for ref in rest[1:]:
        total += ref[...].astype(f32)
    o_ref[n * rows :] = total


def total_corange(done, own, arrived, before):
    rows, *rest = own.shape
    return pl.pallas_call(
        functools.partial(total_kernel, len(done)),
        in_specs=vmem_specs([*done, own, *arrived]) + any_specs([before]),
        out_specs=pl.BlockSpec(memory_space=pltpu.VMEM),
        out_shape=jax.ShapeDtypeStruct((rows * PARTS, *rest), f32),
        name="total_corange",
    )(*done, own, *arrived, before)


def finish_kernel(n_out, n_in, place_ref, *refs):
    o_ref, both_parts = refs[-2:]
    n = n_in // 2 + 1
    i_count = refs[0].shape[0]
    z, idx = place_ref[0], place_ref[1]
    for k, slot in enumerate(slots(n_in)):
        ref, base = min(k, n - 1), max(k - (n - 1), 0) * i_count

        def body(t, _):
            for q in range(PARTS):
                in_order(refs[q * n + ref][base + t], both_parts, q, z, n_out)
            o_ref[(idx ^ slot) * i_count + t] = both_parts[...].T.astype(bf16)
            return 0

        lax.fori_loop(0, i_count, body, 0)


def finish(pieces, place, after, n_out, n_in):
    i_count, s_count, p = pieces[0][0].shape
    flat = [x for part in pieces for x in part]
    return pl.pallas_call(
        functools.partial(finish_kernel, n_out, n_in),
        in_specs=[pl.BlockSpec(memory_space=pltpu.SMEM)] + vmem_specs(flat) + any_specs(after),
        out_specs=pl.BlockSpec(memory_space=pltpu.VMEM),
        out_shape=jax.ShapeDtypeStruct((R, p, PARTS * s_count), bf16),
        scratch_shapes=[pltpu.VMEM((PARTS * s_count, p), f32)],
        compiler_params=pltpu.CompilerParams(vmem_limit_bytes=VMEM),
        cost_estimate=pl.CostEstimate(
            flops=0, bytes_accessed=64 * R * p * s_count, transcendentals=0
        ),
        name="finish",
    )(place, *flat, *after)


def slots(n):
    return [*range(0, n, 2), *range(1, n, 2)]


def to_xor(x, axis, r, n):
    return lax.ppermute(x, axis, [(d, d ^ r) for d in range(n)])


def sum_by_xor(x, axis, n):
    step = 1
    while step < n:
        if 4 * step <= n:
            a, b, c = [to_xor(x, axis, k * step, n) for k in (1, 2, 3)]
            x = (x + a) + (b + c)
            step *= 4
        else:
            x = x + to_xor(x, axis, step, n)
            step *= 2
    return x


def settle_kernel(n, keep_ref, away_ref, *refs):
    total = keep_ref[...] + away_ref[...].astype(f32)
    for ref in refs[:n]:
        total += ref[...].astype(f32)
    refs[-1][...] = total.astype(bf16)


def settle(keep, away, arrived, before):
    block = pl.BlockSpec(arrived[0].shape, lambda i: (0, 0, 0))
    return pl.pallas_call(
        functools.partial(settle_kernel, len(arrived)),
        grid=(1,),
        in_specs=[block] * (2 + len(arrived)) + any_specs(before),
        out_specs=block,
        out_shape=jax.ShapeDtypeStruct(arrived[0].shape, bf16),
        compiler_params=pltpu.CompilerParams(vmem_limit_bytes=VMEM),
        cost_estimate=pl.CostEstimate(
            flops=0, bytes_accessed=8 * arrived[0].size, transcendentals=0
        ),
        name="settle",
    )(keep, away, *arrived, *before)


def meet(keep, send, n):
    away = to_xor(send, "in", 1, n)
    g = R // n
    arrived = []
    for k in range(1, n // 2):
        rows = slice(k * g, (k + 1) * g)
        arrived.append(to_xor((keep[rows] + away[rows].astype(f32)).astype(bf16), "in", 2 * k, n))
    return keep, away, arrived


def spread(own, n):
    return [own] + [to_xor(own, "in", 2 * k, n) for k in range(1, n // 2)]


def join_kernel(n, *refs):
    rows = refs[0].shape[0]
    for k in range(n):
        refs[-1][k * rows : (k + 1) * rows] = refs[k][...]


def join(mine, before):
    rows, *rest = mine[0].shape
    return pl.pallas_call(
        functools.partial(join_kernel, len(mine)),
        in_specs=vmem_specs(mine) + any_specs(before),
        out_specs=pl.BlockSpec(memory_space=pltpu.VMEM),
        out_shape=jax.ShapeDtypeStruct((len(mine) * rows, *rest), bf16),
        name="join",
    )(*mine, *before)


def shards(n_out, n_in, mats, markov, probes, pattern):
    lag_mat, probe_mat, sketch_mat, raw_mat, cor_mat = [jnp.asarray(a) for a in mats]
    rows = probes.shape[0] // PARTS
    z, idx = lax.axis_index("out"), lax.axis_index("in")

    place = jnp.stack([z, idx]).astype(jnp.int32)
    keep = jnp.repeat(pattern, BI, axis=1).astype(f32)[:, None, :]

    own = probes[:rows]
    gathered = [own]
    for d in range(1, n_out):
        gathered.append(lax.ppermute(own, "out", [((k + d) % n_out, k) for k in range(n_out)]))
    for q in range(1, PARTS):
        gathered.append(lax.all_gather(probes[q * rows : (q + 1) * rows], "out"))
    hankel = [lag_transform(markov, keep, lag_mat, q) for q in range(MARKOV_PARTS)]

    raws = sketch_part(gathered, hankel, probe_mat, raw_mat, place, n_out, n_in)
    met = [meet(raws[2 * q], raws[2 * q + 1], n_in) for q in range(PARTS)]
    owns = [settle(*x, []) for x in met]
    joined, sums, summed, before = [], [], [], owns[-1:]
    for q, own in enumerate(owns):
        mine = spread(own, n_in)
        joined.append(join(mine, before if q else []))
        sums.append(mine + [to_xor(joined[q], "in", 1, n_in)])
        last = q == PARTS - 1
        cor = corange_part(
            sums[q], hankel, sketch_mat, cor_mat, place, n_out, n_in, before, not last
        )
        before = [cor[-1]]
        if not last:
            whole = cor[0].reshape((-1,) + cor[0].shape[2:])
            summed.append(lax.psum_scatter(whole, "out", scatter_dimension=0, tiled=True))

    arrived = [
        lax.ppermute(cor[d], "out", [(k, (k + d) % n_out) for k in range(n_out)])
        for d in range(1, n_out)
    ]
    gram = gram_part(joined, place, n_out)
    gram = sum_by_xor(gram + to_xor(gram, "in", 1, n_in), "out", n_out)
    gram_matrix = gram / (R * OUTPUT_CHANNELS)
    sketch = finish(sums, place, [*before, gram_matrix], n_out, n_in)
    corange = total_corange(summed, cor[0], arrived, sketch)
    return (sketch, corange, gram_matrix)


def solution(mesh):
    body = functools.partial(shards, mesh.shape["out"], mesh.shape["in"], constants())
    return jax.shard_map(
        body,
        mesh=mesh,
        in_specs=(P(None, "out", "in"), P("out", None, "in"), P("out", "in")),
        out_specs=(P(None, "out", None), P("out", None, "in"), P()),
        check_vma=False,
    )
```

```python
import functools

import jax
import jax.numpy as jnp
import ml_dtypes
import numpy as np
from jax import lax
from jax.experimental import pallas as pl
from jax.experimental.pallas import tpu as pltpu
from jax.sharding import PartitionSpec as P

OUTPUT_CHANNELS = 2048
BO = 64
BI = 128
R = 32
C = 32
LAGS = 63
F = 32
PARTS = 2
MARKOV_PARTS = 1
CHUNK = 4
VMEM = 60 << 20

bf16 = jnp.bfloat16
f32 = jnp.float32


def split(a):
    hi = a.astype(ml_dtypes.bfloat16)
    lo = (a - hi.astype(np.float64)).astype(ml_dtypes.bfloat16)
    return np.concatenate([hi, lo], axis=0)


def constants():
    theta = np.pi * (2 * np.arange(F)[:, None] + 1) / 64
    lag = np.arange(64)[None]
    cos, sin = np.cos(theta * lag), np.sin(theta * lag)
    eye = np.eye(8)
    fwd = np.stack([cos, sin])
    lag_mat = np.einsum("cfk,pq->cfpkq", fwd, eye).reshape(2 * F * 8, 64 * 8)
    half = fwd[:, :, :32]
    probe_mat = np.einsum("cfj,pq->cfpqj", half, eye).reshape(2 * F * 8, 32 * 8)
    sketch_mat = np.einsum("cfj,pq->cfpjq", half, eye).reshape(2 * F * 8, 32 * 8)
    back = half / F
    raw_mat = np.einsum("cfi,pq->ipcfq", back, eye).reshape(32 * 8, 2 * F * 8)
    cor_mat = np.einsum("cfj,pq->pjcfq", back, eye).reshape(32 * 8, 2 * F * 8)
    return [split(a) for a in (lag_mat, probe_mat, sketch_mat, raw_mat, cor_mat)]


def both(mat_ref, x):
    y = jnp.dot(mat_ref[...], x, preferred_element_type=f32)
    n = y.shape[0] // 2
    return y[:n] + y[n:]


def lag_kernel(keep_ref, mat_ref, x_ref, o_ref):
    rows, m = x_ref.shape[1], x_ref.shape[2]
    keep = keep_ref[0].astype(f32)

    def body(b, _):
        at = pl.ds(pl.multiple_of(b * 16, 16), 16)
        x = x_ref[:, at, :].astype(f32) * keep[None]
        res = []
        for h in range(2):
            part = x[:, 8 * h : 8 * h + 8, :].reshape(LAGS * 8, m)
            part = jnp.concatenate([part, jnp.zeros((8, m), f32)], axis=0)
            res.append(both(mat_ref, part.astype(bf16)).reshape(2, F, 8, m))
        y = jnp.concatenate(res, axis=2).astype(bf16)
        o_ref[:, at, 0:m] = y[0]
        o_ref[:, at, m : 2 * m] = y[1]
        return 0

    lax.fori_loop(0, rows // 16, body, 0)


def lag_transform(markov, keep, mat, part):
    lags, p, m = markov.shape
    blocks = p // BO // MARKOV_PARTS
    return pl.pallas_call(
        lag_kernel,
        grid=(blocks,),
        in_specs=[
            pl.BlockSpec((1, 1, m), lambda i: (part * blocks + i, 0, 0)),
            pl.BlockSpec(mat.shape, lambda i: (0, 0)),
            pl.BlockSpec((lags, BO, m), lambda i: (0, part * blocks + i, 0)),
        ],
        out_specs=pl.BlockSpec((F, BO, 2 * m), lambda i: (0, i, 0)),
        out_shape=jax.ShapeDtypeStruct((F, p // MARKOV_PARTS, 2 * m), bf16),
        compiler_params=pltpu.CompilerParams(vmem_limit_bytes=VMEM),
        cost_estimate=pl.CostEstimate(
            flops=p * m * 1024 * 64, bytes_accessed=2 * 64 * p * m, transcendentals=0
        ),
        name="lag_transform",
    )(keep, mat, markov)


def rotate_into(hat_ref, y, at, at2, lo, hi):
    c, s = y[0].astype(bf16), y[1].astype(bf16)
    hat_ref[:, at, lo] = c
    hat_ref[:, at2, hi] = c
    hat_ref[:, at, hi] = s
    hat_ref[:, at2, lo] = -s


def fetch(m_hbms, m_ref, sems):
    rows = m_ref.shape[1] // MARKOV_PARTS

    def copies(c):
        at = pl.ds(c * CHUNK, CHUNK)
        return [
            pltpu.make_async_copy(
                m_hbm.at[at], m_ref.at[at, pl.ds(k * rows, rows)], sems.at[k, c]
            )
            for k, m_hbm in enumerate(m_hbms)
        ]

    for c in range(F // CHUNK):
        for copy in copies(c):
            copy.start()
    return copies


def over_frequencies(copies, one):
    def body(c, _):
        for copy in copies(c):
            copy.wait()
        for k in range(CHUNK):
            one(c * CHUNK + k)
        return 0

    lax.fori_loop(0, F // CHUNK, body, 0)


def back_input(freq, b, h, s_count, cols):
    re = freq[:, pl.ds(pl.multiple_of(b * 16 + 8 * h, 8), 8), cols]
    im = freq[:, pl.ds(pl.multiple_of(s_count + b * 16 + 8 * h, 8), 8), cols]
    x = jnp.concatenate([re, im], axis=0)
    return x.reshape(2 * F * 8, x.shape[-1]).astype(bf16)


def sketch_kernel(n, n_out, n_in, place_ref, fwd_ref, back_ref, *refs):
    u_refs, m_hbms, refs = refs[:n], refs[n : n + MARKOV_PARTS], refs[n + MARKOV_PARTS :]
    sums, (back, m_ref, hat, freq, sems) = refs[: 2 * PARTS], refs[2 * PARTS :]
    whole = u_refs[n_out:]
    u_refs = list(u_refs[:n_out])
    for ref in whole:
        u_refs += [ref.at[lax.rem(place_ref[0] + d, n_out)] for d in range(n_out)]
    rows, _, m = u_refs[0].shape
    s_count, p = n_out * PARTS * rows, m_ref.shape[1]
    copies = fetch(m_hbms, m_ref, sems)

    for b in range(s_count // 16):
        res = []
        for g in (2 * b, 2 * b + 1):
            first = (g * 8) % rows
            x = u_refs[g * 8 // rows][first : first + 8].reshape(8 * C, m)
            res.append(both(fwd_ref, x).reshape(2, F, 8, m))
        y = jnp.concatenate(res, axis=2)
        at, at2 = pl.ds(b * 16, 16), pl.ds(s_count + b * 16, 16)
        rotate_into(hat, y, at, at2, slice(0, m), slice(m, 2 * m))

    def one(f):
        freq[f] = lax.dot_general(
            hat[f], m_ref[f], (((1,), (1,)), ((), ())), preferred_element_type=f32
        )

    over_frequencies(copies, one)
    width = min(p, 256)
    g = R // n_in * 8
    for part in range(2):
        for k, slot in enumerate(slots(n_in)):
            at = pl.ds(pl.multiple_of(part * R * 8 + (place_ref[1] ^ slot) * g, 16), g)
            back[part * R * 8 + k * g : part * R * 8 + (k + 1) * g] = back_ref[at]

    for q in range(PARTS):
        keep_ref, send_ref = sums[2 * q : 2 * q + 2]
        part = s_count // PARTS // 16

        def body(b, _):
            at = pl.ds(pl.multiple_of(b * 16, 16), 16)
            for w in range(p // width):
                cols = slice(w * width, (w + 1) * width)
                res = []
                for h in range(2):
                    x = back_input(freq, q * part + b, h, s_count, cols)
                    res.append(both(back, x).reshape(R, 8, width))
                y = jnp.concatenate(res, axis=1)
                keep_ref[:, at, cols] = y[: R // 2]
                send_ref[:, at, cols] = y[R // 2 :].astype(bf16)
            return 0

        lax.fori_loop(0, part, body, 0)


def vmem_specs(arrays):
    return [pl.BlockSpec(memory_space=pltpu.VMEM) for _ in arrays]


def any_specs(arrays):
    return [pl.BlockSpec(memory_space=pl.ANY) for _ in arrays]


def product_cost(p, m, extra):
    return pl.CostEstimate(
        flops=2 * F * 256 * 2 * m * p * 2, bytes_accessed=4 * F * p * m + extra, transcendentals=0
    )


def sketch_part(probes, hankel, fwd, back, place, n_out, n_in):
    rows, _, m = probes[0].shape
    p = hankel[0].shape[1] * MARKOV_PARTS
    part, s_count = rows * n_out, rows * n_out * PARTS
    return pl.pallas_call(
        functools.partial(sketch_kernel, len(probes), n_out, n_in),
        in_specs=[pl.BlockSpec(memory_space=pltpu.SMEM)]
        + vmem_specs([fwd, back, *probes])
        + any_specs(hankel),
        out_specs=vmem_specs(range(2 * PARTS)),
        out_shape=[
            jax.ShapeDtypeStruct((R // 2, part, p), f32),
            jax.ShapeDtypeStruct((R // 2, part, p), bf16),
        ]
        * PARTS,
        scratch_shapes=[
            pltpu.VMEM(back.shape, bf16),
            pltpu.VMEM((F, p, 2 * m), bf16),
            pltpu.VMEM((F, 2 * s_count, 2 * m), bf16),
            pltpu.VMEM((F, 2 * s_count, p), f32),
            pltpu.SemaphoreType.DMA((MARKOV_PARTS, F // CHUNK)),
        ],
        compiler_params=pltpu.CompilerParams(vmem_limit_bytes=VMEM),
        cost_estimate=product_cost(p, m, 0),
        name="sketch_part",
    )(place, fwd, back, *probes, *hankel)


def corange_kernel(n_in, n_out, n_before, n_o, place_ref, fwd_ref, back_ref, *refs):
    k_refs, refs = refs[: n_in // 2 + 1], refs[n_in // 2 + 1 :]
    m_hbms, refs = refs[:MARKOV_PARTS], refs[MARKOV_PARTS + n_before :]
    o_refs, (fwd, m_ref, hat, freq, sems) = refs[:n_o], refs[n_o:]
    if n_o == 1:
        o_refs = [o_refs[0].at[lax.rem(place_ref[0] + d, n_out)] for d in range(n_out)]
    _, s_count, p = k_refs[0].shape
    m = m_ref.shape[2] // 2
    rows = s_count // n_out
    copies = fetch(m_hbms, m_ref, sems)
    width = min(p, 256)

    g = R // n_in * 8
    to = lax.broadcasted_iota(jnp.int32, (R * 8, R * 8), 1)
    come = lax.broadcasted_iota(jnp.int32, (R * 8, R * 8), 0)
    where = to // g
    slot = jnp.where(where < n_in // 2, 2 * where, 2 * where - (n_in - 1))
    moved = come == (place_ref[1] ^ slot) * g + to % g
    move = jnp.where(moved, 1.0, 0.0).astype(bf16)
    fwd[...] = jnp.dot(fwd_ref[...], move, preferred_element_type=f32).astype(bf16)

    def forward(b, _):
        at = pl.ds(pl.multiple_of(b * 16, 16), 16)
        at2 = pl.ds(pl.multiple_of(s_count + b * 16, 16), 16)
        for w in range(p // width):
            cols = slice(w * width, (w + 1) * width)
            k = jnp.concatenate([ref[:, at, cols] for ref in k_refs], axis=0).astype(f32)
            res = []
            for h in range(2):
                x = k[:, 8 * h : 8 * h + 8, :].reshape(R * 8, width).astype(bf16)
                res.append(both(fwd, x).reshape(2, F, 8, width))
            y = jnp.concatenate(res, axis=2)
            lo = slice(w * width, (w + 1) * width)
            hi = slice(p + w * width, p + (w + 1) * width)
            rotate_into(hat, y, at, at2, lo, hi)
        return 0

    lax.fori_loop(0, s_count // 16, forward, 0)

    def one(f):
        left = hat[f]
        freq[f] = jnp.dot(left[:, :p], m_ref[f, :, :m], preferred_element_type=f32) + jnp.dot(
            left[:, p:], m_ref[f, :, m:], preferred_element_type=f32
        )

    over_frequencies(copies, one)

    for g in range(s_count // 8):
        x = back_input(freq, g // 2, g % 2, s_count, slice(0, m))
        first = (g * 8) % rows
        o_ref = o_refs[g * 8 // rows]
        o_ref[first : first + 8] = both(back_ref, x).reshape(8, C, m).astype(o_ref.dtype)


def corange_part(pieces, hankel, fwd, back, place, n_out, n_in, before, whole):
    _, s_count, p = pieces[0].shape
    m = hankel[0].shape[2] // 2
    rows = s_count // n_out
    if whole:
        outs = [jax.ShapeDtypeStruct((n_out, rows, C, m), bf16)]
    else:
        outs = [jax.ShapeDtypeStruct((rows, C, m), bf16 if d else f32) for d in range(n_out)]
    return pl.pallas_call(
        functools.partial(corange_kernel, n_in, n_out, len(before), len(outs)),
        in_specs=[pl.BlockSpec(memory_space=pltpu.SMEM)]
        + vmem_specs([fwd, back, *pieces])
        + any_specs([*hankel, *before]),
        out_specs=vmem_specs(outs),
        out_shape=outs,
        scratch_shapes=[
            pltpu.VMEM(fwd.shape, bf16),
            pltpu.VMEM((F, p, 2 * m), bf16),
            pltpu.VMEM((F, 2 * s_count, 2 * p), bf16),
            pltpu.VMEM((F, 2 * s_count, m), f32),
            pltpu.SemaphoreType.DMA((MARKOV_PARTS, F // CHUNK)),
        ],
        compiler_params=pltpu.CompilerParams(vmem_limit_bytes=VMEM),
        cost_estimate=product_cost(p, m, 0),
        name="corange_part",
    )(place, fwd, back, *pieces, *hankel, *before)


def in_order(x, both_parts, q, z, n_out):
    rows = x.shape[0] // n_out
    x = x.astype(f32)
    for d in range(n_out):
        first = lax.rem(z + d, n_out) * (PARTS * rows) + q * rows
        both_parts[pl.ds(pl.multiple_of(first, 8), rows), :] = x[d * rows : (d + 1) * rows]


def gram_kernel(n_out, place_ref, *refs):
    k_refs, (gram_ref, moved) = refs[:PARTS], refs[PARTS:]
    s_count = k_refs[0].shape[1]
    total = jnp.zeros(gram_ref.shape, f32)
    for i in range(k_refs[0].shape[0]):
        x = jnp.concatenate([ref[i] for ref in k_refs], axis=0)
        total += lax.dot_general(x, x, (((1,), (1,)), ((), ())), preferred_element_type=f32)
    for _ in range(2):
        for q in range(PARTS):
            in_order(total[q * s_count : (q + 1) * s_count], moved, q, place_ref[0], n_out)
        total = moved[...].T
    gram_ref[...] = total


def gram_part(joined, place, n_out):
    s_count = PARTS * joined[0].shape[1]
    return pl.pallas_call(
        functools.partial(gram_kernel, n_out),
        in_specs=[pl.BlockSpec(memory_space=pltpu.SMEM)] + vmem_specs(joined),
        out_specs=pl.BlockSpec(memory_space=pltpu.VMEM),
        out_shape=jax.ShapeDtypeStruct((s_count, s_count), f32),
        scratch_shapes=[pltpu.VMEM((s_count, s_count), f32)],
        compiler_params=pltpu.CompilerParams(vmem_limit_bytes=VMEM),
        name="gram_part",
    )(place, *joined)


def total_kernel(n, *refs):
    done, rest, o_ref = refs[:n], refs[n:-2], refs[-1]
    rows = rest[0].shape[0]
    for q, ref in enumerate(done):
        o_ref[q * rows : (q + 1) * rows] = ref[...].astype(f32)
    total = rest[0][...]
    for ref in rest[1:]:
        total += ref[...].astype(f32)
    o_ref[n * rows :] = total


def total_corange(done, own, arrived, before):
    rows, *rest = own.shape
    return pl.pallas_call(
        functools.partial(total_kernel, len(done)),
        in_specs=vmem_specs([*done, own, *arrived]) + any_specs([before]),
        out_specs=pl.BlockSpec(memory_space=pltpu.VMEM),
        out_shape=jax.ShapeDtypeStruct((rows * PARTS, *rest), f32),
        name="total_corange",
    )(*done, own, *arrived, before)


def finish_kernel(n_out, n_in, place_ref, *refs):
    o_ref, both_parts = refs[-2:]
    n = n_in // 2 + 1
    i_count = refs[0].shape[0]
    z, idx = place_ref[0], place_ref[1]
    for k, slot in enumerate(slots(n_in)):
        ref, base = min(k, n - 1), max(k - (n - 1), 0) * i_count

        def body(t, _):
            for q in range(PARTS):
                in_order(refs[q * n + ref][base + t], both_parts, q, z, n_out)
            o_ref[(idx ^ slot) * i_count + t] = both_parts[...].T.astype(bf16)
            return 0

        lax.fori_loop(0, i_count, body, 0)


def finish(pieces, place, after, n_out, n_in):
    i_count, s_count, p = pieces[0][0].shape
    flat = [x for part in pieces for x in part]
    return pl.pallas_call(
        functools.partial(finish_kernel, n_out, n_in),
        in_specs=[pl.BlockSpec(memory_space=pltpu.SMEM)] + vmem_specs(flat) + any_specs(after),
        out_specs=pl.BlockSpec(memory_space=pltpu.VMEM),
        out_shape=jax.ShapeDtypeStruct((R, p, PARTS * s_count), bf16),
        scratch_shapes=[pltpu.VMEM((PARTS * s_count, p), f32)],
        compiler_params=pltpu.CompilerParams(vmem_limit_bytes=VMEM),
        cost_estimate=pl.CostEstimate(
            flops=0, bytes_accessed=64 * R * p * s_count, transcendentals=0
        ),
        name="finish",
    )(place, *flat, *after)


def slots(n):
    return [*range(0, n, 2), *range(1, n, 2)]


def to_xor(x, axis, r, n):
    return lax.ppermute(x, axis, [(d, d ^ r) for d in range(n)])


def sum_by_xor(x, axis, n):
    step = 1
    while step < n:
        if 4 * step <= n:
            a, b, c = [to_xor(x, axis, k * step, n) for k in (1, 2, 3)]
            x = (x + a) + (b + c)
            step *= 4
        else:
            x = x + to_xor(x, axis, step, n)
            step *= 2
    return x


def settle(keep, away, arrived):
    rows = arrived[0].shape[0]
    total = keep[:rows] + away[:rows].astype(f32)
    for x in arrived:
        total = total + x.astype(f32)
    return total.astype(bf16)


def meet(keep, send, n):
    away = to_xor(send, "in", 1, n)
    g = R // n
    arrived = []
    for k in range(1, n // 2):
        rows = slice(k * g, (k + 1) * g)
        arrived.append(to_xor((keep[rows] + away[rows].astype(f32)).astype(bf16), "in", 2 * k, n))
    return keep, away, arrived


def spread(own, n):
    return [own] + [to_xor(own, "in", 2 * k, n) for k in range(1, n // 2)]


def join_kernel(n, *refs):
    rows = refs[0].shape[0]
    for k in range(n):
        refs[-1][k * rows : (k + 1) * rows] = refs[k][...]


def join(mine, before):
    rows, *rest = mine[0].shape
    return pl.pallas_call(
        functools.partial(join_kernel, len(mine)),
        in_specs=vmem_specs(mine) + any_specs(before),
        out_specs=pl.BlockSpec(memory_space=pltpu.VMEM),
        out_shape=jax.ShapeDtypeStruct((len(mine) * rows, *rest), bf16),
        name="join",
    )(*mine, *before)


def shards(n_out, n_in, mats, markov, probes, pattern):
    lag_mat, probe_mat, sketch_mat, raw_mat, cor_mat = [jnp.asarray(a) for a in mats]
    rows = probes.shape[0] // PARTS
    z, idx = lax.axis_index("out"), lax.axis_index("in")

    place = jnp.stack([z, idx]).astype(jnp.int32)
    keep = jnp.repeat(pattern, BI, axis=1).astype(f32)[:, None, :]

    own = probes[:rows]
    gathered = [own]
    for d in range(1, n_out):
        gathered.append(lax.ppermute(own, "out", [((k + d) % n_out, k) for k in range(n_out)]))
    for q in range(1, PARTS):
        gathered.append(lax.all_gather(probes[q * rows : (q + 1) * rows], "out"))
    hankel = [lag_transform(markov, keep, lag_mat, q) for q in range(MARKOV_PARTS)]

    raws = sketch_part(gathered, hankel, probe_mat, raw_mat, place, n_out, n_in)
    met = [meet(raws[2 * q], raws[2 * q + 1], n_in) for q in range(PARTS)]
    owns = [settle(*x) for x in met]
    joined, sums, summed, before = [], [], [], owns[-1:]
    for q, own in enumerate(owns):
        mine = spread(own, n_in)
        joined.append(join(mine, before) if q else jnp.concatenate(mine, axis=0))
        sums.append(mine + [to_xor(joined[q], "in", 1, n_in)])
        last = q == PARTS - 1
        cor = corange_part(
            sums[q], hankel, sketch_mat, cor_mat, place, n_out, n_in, before, not last
        )
        before = [cor[-1]]
        if not last:
            whole = cor[0].reshape((-1,) + cor[0].shape[2:])
            summed.append(lax.psum_scatter(whole, "out", scatter_dimension=0, tiled=True))

    arrived = [
        lax.ppermute(cor[d], "out", [(k, (k + d) % n_out) for k in range(n_out)])
        for d in range(1, n_out)
    ]
    gram = gram_part(joined, place, n_out)
    gram = sum_by_xor(gram + to_xor(gram, "in", 1, n_in), "out", n_out)
    gram_matrix = gram / (R * OUTPUT_CHANNELS)
    sketch = finish(sums, place, [*before, gram_matrix], n_out, n_in)
    corange = total_corange(summed, cor[0], arrived, sketch)
    return (sketch, corange, gram_matrix)


def solution(mesh):
    body = functools.partial(shards, mesh.shape["out"], mesh.shape["in"], constants())
    return jax.shard_map(
        body,
        mesh=mesh,
        in_specs=(P(None, "out", "in"), P("out", None, "in"), P("out", "in")),
        out_specs=(P(None, "out", None), P("out", None, "in"), P()),
        check_vma=False,
    )
```

```python
import functools

import jax
import jax.numpy as jnp
import ml_dtypes
import numpy as np
from jax import lax
from jax.experimental import pallas as pl
from jax.experimental.pallas import tpu as pltpu
from jax.sharding import PartitionSpec as P

OUTPUT_CHANNELS = 2048
BO = 64
BI = 128
R = 32
C = 32
LAGS = 63
F = 32
PARTS = 2
MARKOV_PARTS = 1
CHUNK = 4
VMEM = 60 << 20

bf16 = jnp.bfloat16
f32 = jnp.float32


def split(a):
    hi = a.astype(ml_dtypes.bfloat16)
    lo = (a - hi.astype(np.float64)).astype(ml_dtypes.bfloat16)
    return np.concatenate([hi, lo], axis=0)


def constants():
    theta = np.pi * (2 * np.arange(F)[:, None] + 1) / 64
    lag = np.arange(64)[None]
    cos, sin = np.cos(theta * lag), np.sin(theta * lag)
    eye = np.eye(8)
    fwd = np.stack([cos, sin])
    lag_mat = np.einsum("cfk,pq->cfpkq", fwd, eye).reshape(2 * F * 8, 64 * 8)
    half = fwd[:, :, :32]
    probe_mat = np.einsum("cfj,pq->cfpqj", half, eye).reshape(2 * F * 8, 32 * 8)
    sketch_mat = np.einsum("cfj,pq->cfpjq", half, eye).reshape(2 * F * 8, 32 * 8)
    back = half / F
    raw_mat = np.einsum("cfi,pq->ipcfq", back, eye).reshape(32 * 8, 2 * F * 8)
    cor_mat = np.einsum("cfj,pq->pjcfq", back, eye).reshape(32 * 8, 2 * F * 8)
    return [split(a) for a in (lag_mat, probe_mat, sketch_mat, raw_mat, cor_mat)]


def both(mat_ref, x):
    n = mat_ref.shape[0] // 2
    hi = jnp.dot(mat_ref[:n], x, preferred_element_type=f32)
    return hi + jnp.dot(mat_ref[n:], x, preferred_element_type=f32)


def lag_kernel(keep_ref, mat_ref, x_ref, o_ref):
    rows, m = x_ref.shape[1], x_ref.shape[2]
    keep = keep_ref[0].astype(f32)

    def body(b, _):
        at = pl.ds(pl.multiple_of(b * 16, 16), 16)
        x = x_ref[:, at, :].astype(f32) * keep[None]
        res = []
        for h in range(2):
            part = x[:, 8 * h : 8 * h + 8, :].reshape(LAGS * 8, m)
            part = jnp.concatenate([part, jnp.zeros((8, m), f32)], axis=0)
            res.append(both(mat_ref, part.astype(bf16)).reshape(2, F, 8, m))
        y = jnp.concatenate(res, axis=2).astype(bf16)
        o_ref[:, at, 0:m] = y[0]
        o_ref[:, at, m : 2 * m] = y[1]
        return 0

    lax.fori_loop(0, rows // 16, body, 0)


def lag_transform(markov, keep, mat, part):
    lags, p, m = markov.shape
    blocks = p // BO // MARKOV_PARTS
    return pl.pallas_call(
        lag_kernel,
        grid=(blocks,),
        in_specs=[
            pl.BlockSpec((1, 1, m), lambda i: (part * blocks + i, 0, 0)),
            pl.BlockSpec(mat.shape, lambda i: (0, 0)),
            pl.BlockSpec((lags, BO, m), lambda i: (0, part * blocks + i, 0)),
        ],
        out_specs=pl.BlockSpec((F, BO, 2 * m), lambda i: (0, i, 0)),
        out_shape=jax.ShapeDtypeStruct((F, p // MARKOV_PARTS, 2 * m), bf16),
        compiler_params=pltpu.CompilerParams(vmem_limit_bytes=VMEM),
        cost_estimate=pl.CostEstimate(
            flops=p * m * 1024 * 64, bytes_accessed=2 * 64 * p * m, transcendentals=0
        ),
        name="lag_transform",
    )(keep, mat, markov)


def rotate_into(hat_ref, y, at, at2, lo, hi):
    c, s = y[0].astype(bf16), y[1].astype(bf16)
    hat_ref[:, at, lo] = c
    hat_ref[:, at2, hi] = c
    hat_ref[:, at, hi] = s
    hat_ref[:, at2, lo] = -s


def fetch(m_hbms, m_ref, sems):
    rows = m_ref.shape[1] // MARKOV_PARTS

    def copies(c):
        at = pl.ds(c * CHUNK, CHUNK)
        return [
            pltpu.make_async_copy(
                m_hbm.at[at], m_ref.at[at, pl.ds(k * rows, rows)], sems.at[k, c]
            )
            for k, m_hbm in enumerate(m_hbms)
        ]

    for c in range(F // CHUNK):
        for copy in copies(c):
            copy.start()
    return copies


def over_frequencies(copies, one):
    def body(c, _):
        for copy in copies(c):
            copy.wait()
        for k in range(CHUNK):
            one(c * CHUNK + k)
        return 0

    lax.fori_loop(0, F // CHUNK, body, 0)


def back_input(freq, b, h, s_count, cols):
    re = freq[:, pl.ds(pl.multiple_of(b * 16 + 8 * h, 8), 8), cols]
    im = freq[:, pl.ds(pl.multiple_of(s_count + b * 16 + 8 * h, 8), 8), cols]
    x = jnp.concatenate([re, im], axis=0)
    return x.reshape(2 * F * 8, x.shape[-1]).astype(bf16)


def sketch_kernel(n, n_out, n_in, place_ref, fwd_ref, back_ref, *refs):
    u_refs, m_hbms, refs = refs[:n], refs[n : n + MARKOV_PARTS], refs[n + MARKOV_PARTS :]
    sums, (back, m_ref, hat, freq, sems) = refs[: 2 * PARTS], refs[2 * PARTS :]
    whole = u_refs[n_out:]
    u_refs = list(u_refs[:n_out])
    for ref in whole:
        u_refs += [ref.at[lax.rem(place_ref[0] + d, n_out)] for d in range(n_out)]
    rows, _, m = u_refs[0].shape
    s_count, p = n_out * PARTS * rows, m_ref.shape[1]
    copies = fetch(m_hbms, m_ref, sems)

    for b in range(s_count // 16):
        res = []
        for g in (2 * b, 2 * b + 1):
            first = (g * 8) % rows
            x = u_refs[g * 8 // rows][first : first + 8].reshape(8 * C, m)
            res.append(both(fwd_ref, x).reshape(2, F, 8, m))
        y = jnp.concatenate(res, axis=2)
        at, at2 = pl.ds(b * 16, 16), pl.ds(s_count + b * 16, 16)
        rotate_into(hat, y, at, at2, slice(0, m), slice(m, 2 * m))

    def one(f):
        freq[f] = lax.dot_general(
            hat[f], m_ref[f], (((1,), (1,)), ((), ())), preferred_element_type=f32
        )

    over_frequencies(copies, one)
    width = min(p, 256)
    g = R // n_in * 8
    for part in range(2):
        for k, slot in enumerate(slots(n_in)):
            at = pl.ds(pl.multiple_of(part * R * 8 + (place_ref[1] ^ slot) * g, 16), g)
            back[part * R * 8 + k * g : part * R * 8 + (k + 1) * g] = back_ref[at]

    for q in range(PARTS):
        keep_ref, send_ref = sums[2 * q : 2 * q + 2]
        part = s_count // PARTS // 16

        def body(b, _):
            at = pl.ds(pl.multiple_of(b * 16, 16), 16)
            for w in range(p // width):
                cols = slice(w * width, (w + 1) * width)
                res = []
                for h in range(2):
                    x = back_input(freq, q * part + b, h, s_count, cols)
                    res.append(both(back, x).reshape(R, 8, width))
                y = jnp.concatenate(res, axis=1)
                keep_ref[:, at, cols] = y[: R // 2]
                send_ref[:, at, cols] = y[R // 2 :].astype(bf16)
            return 0

        lax.fori_loop(0, part, body, 0)


def vmem_specs(arrays):
    return [pl.BlockSpec(memory_space=pltpu.VMEM) for _ in arrays]


def any_specs(arrays):
    return [pl.BlockSpec(memory_space=pl.ANY) for _ in arrays]


def product_cost(p, m, extra):
    return pl.CostEstimate(
        flops=2 * F * 256 * 2 * m * p * 2, bytes_accessed=4 * F * p * m + extra, transcendentals=0
    )


def sketch_part(probes, hankel, fwd, back, place, n_out, n_in):
    rows, _, m = probes[0].shape
    p = hankel[0].shape[1] * MARKOV_PARTS
    part, s_count = rows * n_out, rows * n_out * PARTS
    return pl.pallas_call(
        functools.partial(sketch_kernel, len(probes), n_out, n_in),
        in_specs=[pl.BlockSpec(memory_space=pltpu.SMEM)]
        + vmem_specs([fwd, back, *probes])
        + any_specs(hankel),
        out_specs=vmem_specs(range(2 * PARTS)),
        out_shape=[
            jax.ShapeDtypeStruct((R // 2, part, p), f32),
            jax.ShapeDtypeStruct((R // 2, part, p), bf16),
        ]
        * PARTS,
        scratch_shapes=[
            pltpu.VMEM(back.shape, bf16),
            pltpu.VMEM((F, p, 2 * m), bf16),
            pltpu.VMEM((F, 2 * s_count, 2 * m), bf16),
            pltpu.VMEM((F, 2 * s_count, p), f32),
            pltpu.SemaphoreType.DMA((MARKOV_PARTS, F // CHUNK)),
        ],
        compiler_params=pltpu.CompilerParams(vmem_limit_bytes=VMEM),
        cost_estimate=product_cost(p, m, 0),
        name="sketch_part",
    )(place, fwd, back, *probes, *hankel)


def corange_kernel(n_in, n_out, n_before, n_o, place_ref, fwd_ref, back_ref, *refs):
    k_refs, refs = refs[: n_in // 2 + 1], refs[n_in // 2 + 1 :]
    m_hbms, refs = refs[:MARKOV_PARTS], refs[MARKOV_PARTS + n_before :]
    o_refs, (fwd, m_ref, hat, freq, sems) = refs[:n_o], refs[n_o:]
    if n_o == 1:
        o_refs = [o_refs[0].at[lax.rem(place_ref[0] + d, n_out)] for d in range(n_out)]
    _, s_count, p = k_refs[0].shape
    m = m_ref.shape[2] // 2
    rows = s_count // n_out
    copies = fetch(m_hbms, m_ref, sems)
    width = min(p, 256)

    g = R // n_in * 8
    to = lax.broadcasted_iota(jnp.int32, (R * 8, R * 8), 1)
    come = lax.broadcasted_iota(jnp.int32, (R * 8, R * 8), 0)
    where = to // g
    slot = jnp.where(where < n_in // 2, 2 * where, 2 * where - (n_in - 1))
    moved = come == (place_ref[1] ^ slot) * g + to % g
    move = jnp.where(moved, 1.0, 0.0).astype(bf16)
    fwd[...] = jnp.dot(fwd_ref[...], move, preferred_element_type=f32).astype(bf16)

    def forward(b, _):
        at = pl.ds(pl.multiple_of(b * 16, 16), 16)
        at2 = pl.ds(pl.multiple_of(s_count + b * 16, 16), 16)
        for w in range(p // width):
            cols = slice(w * width, (w + 1) * width)
            k = jnp.concatenate([ref[:, at, cols] for ref in k_refs], axis=0).astype(f32)
            res = []
            for h in range(2):
                x = k[:, 8 * h : 8 * h + 8, :].reshape(R * 8, width).astype(bf16)
                res.append(both(fwd, x).reshape(2, F, 8, width))
            y = jnp.concatenate(res, axis=2)
            lo = slice(w * width, (w + 1) * width)
            hi = slice(p + w * width, p + (w + 1) * width)
            rotate_into(hat, y, at, at2, lo, hi)
        return 0

    lax.fori_loop(0, s_count // 16, forward, 0)

    def one(f):
        left = hat[f]
        freq[f] = jnp.dot(left[:, :p], m_ref[f, :, :m], preferred_element_type=f32) + jnp.dot(
            left[:, p:], m_ref[f, :, m:], preferred_element_type=f32
        )

    over_frequencies(copies, one)

    for g in range(s_count // 8):
        x = back_input(freq, g // 2, g % 2, s_count, slice(0, m))
        first = (g * 8) % rows
        o_ref = o_refs[g * 8 // rows]
        o_ref[first : first + 8] = both(back_ref, x).reshape(8, C, m).astype(o_ref.dtype)


def corange_part(pieces, hankel, fwd, back, place, n_out, n_in, before, whole):
    _, s_count, p = pieces[0].shape
    m = hankel[0].shape[2] // 2
    rows = s_count // n_out
    if whole:
        outs = [jax.ShapeDtypeStruct((n_out, rows, C, m), bf16)]
    else:
        outs = [jax.ShapeDtypeStruct((rows, C, m), bf16 if d else f32) for d in range(n_out)]
    return pl.pallas_call(
        functools.partial(corange_kernel, n_in, n_out, len(before), len(outs)),
        in_specs=[pl.BlockSpec(memory_space=pltpu.SMEM)]
        + vmem_specs([fwd, back, *pieces])
        + any_specs([*hankel, *before]),
        out_specs=vmem_specs(outs),
        out_shape=outs,
        scratch_shapes=[
            pltpu.VMEM(fwd.shape, bf16),
            pltpu.VMEM((F, p, 2 * m), bf16),
            pltpu.VMEM((F, 2 * s_count, 2 * p), bf16),
            pltpu.VMEM((F, 2 * s_count, m), f32),
            pltpu.SemaphoreType.DMA((MARKOV_PARTS, F // CHUNK)),
        ],
        compiler_params=pltpu.CompilerParams(vmem_limit_bytes=VMEM),
        cost_estimate=product_cost(p, m, 0),
        name="corange_part",
    )(place, fwd, back, *pieces, *hankel, *before)


def in_order(x, both_parts, q, z, n_out):
    rows = x.shape[0] // n_out
    x = x.astype(f32)
    for d in range(n_out):
        first = lax.rem(z + d, n_out) * (PARTS * rows) + q * rows
        both_parts[pl.ds(pl.multiple_of(first, 8), rows), :] = x[d * rows : (d + 1) * rows]


def gram_kernel(n_out, place_ref, *refs):
    k_refs, (gram_ref, moved) = refs[:PARTS], refs[PARTS:]
    s_count = k_refs[0].shape[1]
    total = jnp.zeros(gram_ref.shape, f32)
    for i in range(k_refs[0].shape[0]):
        x = jnp.concatenate([ref[i] for ref in k_refs], axis=0)
        total += lax.dot_general(x, x, (((1,), (1,)), ((), ())), preferred_element_type=f32)
    for _ in range(2):
        for q in range(PARTS):
            in_order(total[q * s_count : (q + 1) * s_count], moved, q, place_ref[0], n_out)
        total = moved[...].T
    gram_ref[...] = total


def gram_part(joined, place, n_out):
    s_count = PARTS * joined[0].shape[1]
    return pl.pallas_call(
        functools.partial(gram_kernel, n_out),
        in_specs=[pl.BlockSpec(memory_space=pltpu.SMEM)] + vmem_specs(joined),
        out_specs=pl.BlockSpec(memory_space=pltpu.VMEM),
        out_shape=jax.ShapeDtypeStruct((s_count, s_count), f32),
        scratch_shapes=[pltpu.VMEM((s_count, s_count), f32)],
        compiler_params=pltpu.CompilerParams(vmem_limit_bytes=VMEM),
        name="gram_part",
    )(place, *joined)


def total_kernel(n, *refs):
    done, rest, o_ref = refs[:n], refs[n:-2], refs[-1]
    rows = rest[0].shape[0]
    for q, ref in enumerate(done):
        o_ref[q * rows : (q + 1) * rows] = ref[...].astype(f32)
    total = rest[0][...]
    for ref in rest[1:]:
        total += ref[...].astype(f32)
    o_ref[n * rows :] = total


def total_corange(done, own, arrived, before):
    rows, *rest = own.shape
    return pl.pallas_call(
        functools.partial(total_kernel, len(done)),
        in_specs=vmem_specs([*done, own, *arrived]) + any_specs([before]),
        out_specs=pl.BlockSpec(memory_space=pltpu.VMEM),
        out_shape=jax.ShapeDtypeStruct((rows * PARTS, *rest), f32),
        name="total_corange",
    )(*done, own, *arrived, before)


def finish_kernel(n_out, n_in, place_ref, *refs):
    o_ref, both_parts = refs[-2:]
    n = n_in // 2 + 1
    i_count = refs[0].shape[0]
    z, idx = place_ref[0], place_ref[1]
    for k, slot in enumerate(slots(n_in)):
        ref, base = min(k, n - 1), max(k - (n - 1), 0) * i_count

        def body(t, _):
            for q in range(PARTS):
                in_order(refs[q * n + ref][base + t], both_parts, q, z, n_out)
            o_ref[(idx ^ slot) * i_count + t] = both_parts[...].T.astype(bf16)
            return 0

        lax.fori_loop(0, i_count, body, 0)


def finish(pieces, place, after, n_out, n_in):
    i_count, s_count, p = pieces[0][0].shape
    flat = [x for part in pieces for x in part]
    return pl.pallas_call(
        functools.partial(finish_kernel, n_out, n_in),
        in_specs=[pl.BlockSpec(memory_space=pltpu.SMEM)] + vmem_specs(flat) + any_specs(after),
        out_specs=pl.BlockSpec(memory_space=pltpu.VMEM),
        out_shape=jax.ShapeDtypeStruct((R, p, PARTS * s_count), bf16),
        scratch_shapes=[pltpu.VMEM((PARTS * s_count, p), f32)],
        compiler_params=pltpu.CompilerParams(vmem_limit_bytes=VMEM),
        cost_estimate=pl.CostEstimate(
            flops=0, bytes_accessed=64 * R * p * s_count, transcendentals=0
        ),
        name="finish",
    )(place, *flat, *after)


def slots(n):
    return [*range(0, n, 2), *range(1, n, 2)]


def to_xor(x, axis, r, n):
    return lax.ppermute(x, axis, [(d, d ^ r) for d in range(n)])


def sum_by_xor(x, axis, n):
    step = 1
    while step < n:
        if 4 * step <= n:
            a, b, c = [to_xor(x, axis, k * step, n) for k in (1, 2, 3)]
            x = (x + a) + (b + c)
            step *= 4
        else:
            x = x + to_xor(x, axis, step, n)
            step *= 2
    return x


def settle(keep, away, arrived):
    rows = arrived[0].shape[0]
    total = keep[:rows] + away[:rows].astype(f32)
    for x in arrived:
        total = total + x.astype(f32)
    return total.astype(bf16)


def meet(keep, send, n):
    away = to_xor(send, "in", 1, n)
    g = R // n
    arrived = []
    for k in range(1, n // 2):
        rows = slice(k * g, (k + 1) * g)
        arrived.append(to_xor((keep[rows] + away[rows].astype(f32)).astype(bf16), "in", 2 * k, n))
    return keep, away, arrived


def spread(own, n):
    return [own] + [to_xor(own, "in", 2 * k, n) for k in range(1, n // 2)]


def join_kernel(n, *refs):
    rows = refs[0].shape[0]
    for k in range(n):
        refs[-1][k * rows : (k + 1) * rows] = refs[k][...]


def join(mine, before):
    rows, *rest = mine[0].shape
    return pl.pallas_call(
        functools.partial(join_kernel, len(mine)),
        in_specs=vmem_specs(mine) + any_specs(before),
        out_specs=pl.BlockSpec(memory_space=pltpu.VMEM),
        out_shape=jax.ShapeDtypeStruct((len(mine) * rows, *rest), bf16),
        name="join",
    )(*mine, *before)


def shards(n_out, n_in, mats, markov, probes, pattern):
    lag_mat, probe_mat, sketch_mat, raw_mat, cor_mat = [jnp.asarray(a) for a in mats]
    rows = probes.shape[0] // PARTS
    z, idx = lax.axis_index("out"), lax.axis_index("in")

    place = jnp.stack([z, idx]).astype(jnp.int32)
    keep = jnp.repeat(pattern, BI, axis=1).astype(f32)[:, None, :]

    own = probes[:rows]
    gathered = [own]
    for d in range(1, n_out):
        gathered.append(lax.ppermute(own, "out", [((k + d) % n_out, k) for k in range(n_out)]))
    for q in range(1, PARTS):
        gathered.append(lax.all_gather(probes[q * rows : (q + 1) * rows], "out"))
    hankel = [lag_transform(markov, keep, lag_mat, q) for q in range(MARKOV_PARTS)]

    raws = sketch_part(gathered, hankel, probe_mat, raw_mat, place, n_out, n_in)
    met = [meet(raws[2 * q], raws[2 * q + 1], n_in) for q in range(PARTS)]
    owns = [settle(*x) for x in met]
    joined, sums, summed, before = [], [], [], owns[-1:]
    for q, own in enumerate(owns):
        mine = spread(own, n_in)
        joined.append(join(mine, before) if q else jnp.concatenate(mine, axis=0))
        sums.append(mine + [to_xor(joined[q], "in", 1, n_in)])
        last = q == PARTS - 1
        cor = corange_part(
            sums[q], hankel, sketch_mat, cor_mat, place, n_out, n_in, before, not last
        )
        before = [cor[-1]]
        if not last:
            whole = cor[0].reshape((-1,) + cor[0].shape[2:])
            summed.append(lax.psum_scatter(whole, "out", scatter_dimension=0, tiled=True))

    arrived = [
        lax.ppermute(cor[d], "out", [(k, (k + d) % n_out) for k in range(n_out)])
        for d in range(1, n_out)
    ]
    gram = gram_part(joined, place, n_out)
    gram = sum_by_xor(gram + to_xor(gram, "in", 1, n_in), "out", n_out)
    gram_matrix = gram / (R * OUTPUT_CHANNELS)
    sketch = finish(sums, place, [*before, gram_matrix], n_out, n_in)
    corange = total_corange(summed, cor[0], arrived, sketch)
    return (sketch, corange, gram_matrix)


def solution(mesh):
    body = functools.partial(shards, mesh.shape["out"], mesh.shape["in"], constants())
    return jax.shard_map(
        body,
        mesh=mesh,
        in_specs=(P(None, "out", "in"), P("out", None, "in"), P("out", "in")),
        out_specs=(P(None, "out", None), P("out", None, "in"), P()),
        check_vma=False,
    )
```
